256 devices in a mesh: blk: 128 (over y, x_hi, z, core), rep: 2 (over x_lo).
Axes of the slice: x: 4 (x_hi: 2, x_lo: 2; x = x_hi * 2 + x_lo), y: 4, z: 8, core: 2. Of those that a mesh axis runs over, the one named last changes fastest.
Arguments:
- entities: bfloat16 [65536, 400], P('blk'), may hold values from -1.75 to 1.75
- hot_entities: bfloat16 [1024, 400], replicated, may hold values from -1.75 to 1.75
- relations: bfloat16 [4096, 400], replicated, may hold values from -3.5 to 3.5
- src_ids: int32 [128, 2, 3, 256], P('blk', 'rep'), may hold values from 0 to 511
- rel_ids: int32 [128, 2, 3, 256], P('blk', 'rep'), may hold values from 0 to 4095
- dst_ids: int32 [128, 2, 3, 256], P('blk', 'rep'), may hold values from 0 to 511
- neg_ids: int32 [128, 2, 3, 512], P('blk', 'rep'), may hold values from 0 to 1535
- counts: int32 [128, 2, 3], P('blk', 'rep'), may hold values from 1 to 256, as said below
- hot_slot: int32 [1024], replicated, may hold values from 0 to 1023, each once
Outputs:
- entity_grad: float32 [65536, 400], P('blk')
- relation_grad: float32 [4096, 400], replicated
- hot_grad: float32 [1024, 400], P(('blk', 'rep'))
The draws below stay inside these ranges and needn't reach their ends.
Inputs may be any that keep to these rules, and one draw needn't show every extreme that they name: `counts`: some slot block of every draw is full.
All inputs are finite; a program needn't handle non-finite values.
Results may differ from the reference program's by a relative error of at most 0.0044.
Values may be sent and summed in bfloat16 or wider, within the bound.
No kernel may reach another device: no remote copies, remote signals or barrier semaphores. Data moves between devices by JAX's collectives and lax.ppermute only.
A program may use at most 128 MiB of HBM per device.

```python
import math
import jax
import jax.numpy as jnp
import numpy as np
from jax import lax

D = 400
NREL = 4096
EDGES_SLOT = 256
NEG = 512
ENT_DEV = 512
HALF = 1
BUCKETS = 3
ENTITIES = 65536
HOT = 1024
N_BLK = 128
N_REP = 2


def draw_entities(key, part):
    key = jax.random.fold_in(key, 3)
    values = jnp.clip(0.5 * jax.random.normal(key, (ENTITIES, D), jnp.float32), -1.7, 1.7)
    return values.astype(jnp.bfloat16)


def draw_hot_entities(key, part):
    key = jax.random.fold_in(key, 4)
    values = jnp.clip(0.5 * jax.random.normal(key, (HOT, D), jnp.float32), -1.7, 1.7)
    return values.astype(jnp.bfloat16)


def draw_relations(key, part):
    key = jax.random.fold_in(key, 5)
    values = jnp.clip(jax.random.normal(key, (NREL, D), jnp.float32), -3.5, 3.5)
    return values.astype(jnp.bfloat16)


def draw_counts(key, part):
    key = jax.random.fold_in(key, 7)
    base_key, spot_key = jax.random.split(key)
    total_slots = N_BLK * N_REP * BUCKETS
    base = jax.random.randint(base_key, (total_slots,), EDGES_SLOT // 5, EDGES_SLOT + 1)
    spot = jax.random.randint(spot_key, (), 0, total_slots)
    filled = jnp.where(jnp.arange(total_slots, dtype=jnp.int32) == spot, EDGES_SLOT, base)
    return filled.reshape(N_BLK, N_REP, BUCKETS).astype(jnp.int32)


def touch_ends(values, stream_key, low, largest):
    longest = values.shape.index(max(values.shape))
    spots = []
    for shift in (0, 1):
        where = [jax.random.randint(jax.random.fold_in(stream_key, axis), (), 0, length) for axis, length in enumerate(values.shape)]
        where[longest] = (where[longest] + shift) % values.shape[longest]
        spots.append(tuple(where))
    return values.at[spots[0]].set(low).at[spots[1]].set(largest)


def rank_table(count, skew):
    weights = [(1 << 20) // math.isqrt(grade ** skew) + 1 for grade in range(1, count + 1)]
    scale = 1 + sum(weights) // (1 << 30)
    return np.cumsum(np.array([max(1, weight // scale) for weight in weights]))


def skewed_ids(key, shape, count, slope):
    grid = rank_table(count, slope)
    lot = jax.random.randint(jax.random.fold_in(key, 1), shape, 0, int(grid[count - 1]))
    standing = jnp.searchsorted(jnp.asarray(grid, jnp.int32), lot, side="right")
    return jax.random.permutation(jax.random.fold_in(key, 2), count)[standing].astype(jnp.int32)


def setup_inputs(seed: int = 0) -> dict:
    arg_keys = jax.random.split(jax.random.key(seed), 10)
    entities = draw_entities(jax.random.fold_in(arg_keys[9], 71), 0)
    hot_entities = draw_hot_entities(jax.random.fold_in(arg_keys[9], 71), 0)
    relations = draw_relations(jax.random.fold_in(arg_keys[9], 71), 0)
    src_ids = touch_ends(jax.random.randint(arg_keys[3], (N_BLK, N_REP, BUCKETS, EDGES_SLOT), 0, ENT_DEV), jax.random.fold_in(arg_keys[3], 1), 0, ENT_DEV - 1).astype(jnp.int32)
    rel_ids = touch_ends(skewed_ids(arg_keys[4], (N_BLK, N_REP, BUCKETS, EDGES_SLOT), NREL, 2), jax.random.fold_in(arg_keys[4], 3), 0, NREL - 1).astype(jnp.int32)
    dst_ids = touch_ends(jax.random.randint(arg_keys[5], (N_BLK, N_REP, BUCKETS, EDGES_SLOT), 0, ENT_DEV), jax.random.fold_in(arg_keys[5], 1), 0, ENT_DEV - 1).astype(jnp.int32)
    neg_ids = touch_ends(jax.random.randint(arg_keys[6], (N_BLK, N_REP, BUCKETS, NEG), 0, ENT_DEV + HOT), jax.random.fold_in(arg_keys[6], 1), 0, (ENT_DEV + HOT) - 1).astype(jnp.int32)
    counts = draw_counts(jax.random.fold_in(arg_keys[9], 71), 0)
    hot_slot = jax.random.permutation(arg_keys[8], HOT).astype(jnp.int32)
    return {"entities": entities, "hot_entities": hot_entities, "relations": relations, "src_ids": src_ids, "rel_ids": rel_ids, "dst_ids": dst_ids, "neg_ids": neg_ids, "counts": counts, "hot_slot": hot_slot}


def complex_mul(left_real, left_imag, right_real, right_imag):
    return left_real * right_real - left_imag * right_imag, left_real * right_imag + left_imag * right_real


def edge_grads(src_rows, rel_rows, dst_rows, neg_rows, live_mask):
    width = src_rows.shape[1] // 2
    src_float = src_rows.astype(jnp.float32)
    rel_float = rel_rows.astype(jnp.float32)
    dst_float = dst_rows.astype(jnp.float32)
    src_real, src_imag = src_float[:, :width], src_float[:, width:]
    rel_real, rel_imag = rel_float[:, :width], rel_float[:, width:]
    prod_real, prod_imag = complex_mul(src_real, src_imag, rel_real, rel_imag)
    product = jnp.concatenate([prod_real, prod_imag], axis=1)
    product_low = product.astype(jnp.bfloat16)
    positive = jnp.sum(product * dst_float, axis=1)
    negative = lax.dot_general(product_low, neg_rows, (((1,), (1,)), ((), ())), preferred_element_type=jnp.float32)
    peak_score = jnp.maximum(positive, jnp.max(negative, axis=1))
    exp_positive = jnp.exp(positive - peak_score)
    exp_negative = jnp.exp(negative - peak_score[:, None])
    total_mass = exp_positive + jnp.sum(exp_negative, axis=1)
    g_positive = live_mask * (exp_positive / total_mass - 1.0)
    weights = (live_mask[:, None] * exp_negative / total_mass[:, None]).astype(jnp.bfloat16)
    g_pool = lax.dot_general(weights, product_low, (((0,), (0,)), ((), ())), preferred_element_type=jnp.float32)
    g_product = g_positive[:, None] * dst_float + jnp.dot(weights, neg_rows, preferred_element_type=jnp.float32)
    grad_real, grad_imag = g_product[:, :width], g_product[:, width:]
    source_real, source_imag = complex_mul(grad_real, grad_imag, rel_real, -rel_imag)
    relation_real, relation_imag = complex_mul(grad_real, grad_imag, src_real, -src_imag)
    g_source = jnp.concatenate([source_real, source_imag], axis=1)
    g_relation = jnp.concatenate([relation_real, relation_imag], axis=1)
    g_target = g_positive[:, None] * product
    return g_source, g_relation, g_target, g_pool


def reference(entities, hot_entities, relations, src_ids, rel_ids, dst_ids, neg_ids, counts, hot_slot):
    per_block = N_REP * BUCKETS
    slot_index = jnp.arange(EDGES_SLOT, dtype=jnp.int32)

    def one_bucket(carry, index):
        entity_total, relation_total, hot_total = carry
        partition = index // per_block
        shard = (index % per_block) // BUCKETS
        bucket = index % BUCKETS
        target = (partition + HALF - bucket + N_BLK) % N_BLK
        own_start = (partition * ENT_DEV).astype(jnp.int32)
        far_start = (target * ENT_DEV).astype(jnp.int32)
        far_block = lax.dynamic_slice_in_dim(entities, far_start, ENT_DEV, 0)
        neg_pool = jnp.concatenate([far_block, hot_entities], axis=0)
        src_local = src_ids[partition, shard, bucket]
        rel_local = rel_ids[partition, shard, bucket]
        dst_local = dst_ids[partition, shard, bucket]
        neg_local = neg_ids[partition, shard, bucket]
        live_mask = (slot_index < counts[partition, shard, bucket]).astype(jnp.float32)
        src_rows = entities[(own_start + src_local).astype(jnp.int32)]
        dst_rows = far_block[dst_local]
        g_source, g_relation, g_target, g_pool = edge_grads(src_rows, relations[rel_local], dst_rows, neg_pool[neg_local], live_mask)
        pool_grad = jnp.zeros((ENT_DEV + HOT, D), jnp.float32).at[neg_local].add(g_pool)
        far_grad = pool_grad[:ENT_DEV].at[dst_local].add(g_target)
        entity_total = entity_total.at[(own_start + src_local).astype(jnp.int32)].add(g_source)
        old_far = lax.dynamic_slice_in_dim(entity_total, far_start, ENT_DEV, 0)
        entity_total = lax.dynamic_update_slice_in_dim(entity_total, old_far + far_grad, far_start, 0)
        relation_total = relation_total.at[rel_local].add(g_relation)
        hot_total = hot_total + pool_grad[ENT_DEV:]
        return (entity_total, relation_total, hot_total), None

    start = (jnp.zeros((ENTITIES, D), jnp.float32), jnp.zeros((NREL, D), jnp.float32), jnp.zeros((HOT, D), jnp.float32))
    steps_all = jnp.arange(N_BLK * per_block, dtype=jnp.int32)
    (entity_grad, relation_grad, hot_total), unused = lax.scan(one_bucket, start, steps_all)
    hot_grad = jnp.zeros((HOT, D), jnp.float32).at[hot_slot].set(hot_total)
    return entity_grad, relation_grad, hot_grad
```

```python
import functools
import jax
import jax.numpy as jnp
import numpy as np
from jax import lax
from jax.experimental import pallas as pl
from jax.experimental.pallas import tpu as pltpu
from jax.sharding import Mesh, PartitionSpec as P

F32 = jnp.float32
BF16 = jnp.bfloat16
D = 400
HALF_D = 200
NREL = 4096
EDGES = 256
NEG = 512
ENT = 512
HOT = 1024
PLANE = 16
DEPTH = 8
LANES = 128
REL_ROWS = D + 16
HOT_BASE = 6 * REL_ROWS
HOT_BLOCKS = 4
MSG_ROWS = HOT_BASE + HOT_BLOCKS * 512
SLAB = D + HOT_BLOCKS * 32
Z_REL = 64
Z_ROWS = Z_REL + 16
BLK = ("y", "xh", "z", "core")
YX = ("y", "xh", "rep")


def onehot(rows, ids):
    grid = lax.broadcasted_iota(jnp.int32, (rows, ids.shape[1]), 0)
    return jnp.where(grid == ids, 1.0, 0.0).astype(BF16)


def dot(a, b):
    return lax.dot_general(a, b, (((1,), (0,)), ((), ())), preferred_element_type=F32)


def dot_nt(a, b):
    return lax.dot_general(a, b, (((1,), (1,)), ((), ())), preferred_element_type=F32)


def to_column(row):
    return jnp.transpose(jnp.broadcast_to(row, (8, row.shape[1])))[:, :1]


def to_row(column):
    return jnp.transpose(jnp.broadcast_to(column, (column.shape[0], LANES)))[:1]


def halves(value):
    return value[:HALF_D], value[HALF_D:]


def complex_product(left, right):
    lr, li = halves(left)
    rr, ri = halves(right)
    return jnp.concatenate([lr * rr - li * ri, lr * ri + li * rr], axis=0)


def conj_product(left, right):
    lr, li = halves(left)
    rr, ri = halves(right)
    return jnp.concatenate([lr * rr + li * ri, li * rr - lr * ri], axis=0)


def bucket_grads(src, rel, low, low_t, far, hot, hot_scores, dst, neg, count):
    src = src.astype(F32)
    rel = rel.astype(F32)
    product = complex_product(src, rel)
    dst_hot = onehot(ENT, dst)
    target = dot(far, dst_hot)
    positive = to_column(jnp.sum(product * target, axis=0, keepdims=True))
    neg_hot = onehot(ENT + HOT, neg)
    times = dot_nt(jnp.ones((8, NEG), BF16), neg_hot)[:1]
    bias = jnp.where(times > 0.0, jnp.log(jnp.maximum(times, 1.0)), -1e30)
    score_far = dot(low_t, far) + bias[:, :ENT]
    score_hot = hot_scores + bias[:, ENT:]
    peak = jnp.maximum(
        jnp.max(score_far, axis=1, keepdims=True), jnp.max(score_hot, axis=1, keepdims=True)
    )
    peak = jnp.maximum(peak, positive)
    exp_far = jnp.exp(score_far - peak)
    exp_hot = jnp.exp(score_hot - peak)
    exp_positive = jnp.exp(positive - peak)
    total = (
        exp_positive
        + jnp.sum(exp_far, axis=1, keepdims=True)
        + jnp.sum(exp_hot, axis=1, keepdims=True)
    )
    live = jnp.where(lax.broadcasted_iota(jnp.int32, (EDGES, 1), 0) < count, 1.0, 0.0)
    g_positive = to_row(live * (exp_positive / total - 1.0))
    scale = live / total
    w_far = (exp_far * scale).astype(BF16)
    w_hot = (exp_hot * scale).astype(BF16)
    g_product = g_positive * target + dot_nt(far, w_far) + dot_nt(hot, w_hot)
    g_source = conj_product(g_product, rel).astype(BF16)
    g_relation = conj_product(g_product, src).astype(BF16)
    g_target = (g_positive * product).astype(BF16)
    g_far = dot(low, w_far) + dot_nt(g_target, dst_hot)
    g_hot = dot(low, w_hot)
    return g_source, g_relation, g_far, g_hot


def front_kernel(
    rel_ref, own_ref, hot_ref, src_ref, rid_ref, dst_ref, neg_ref, count_ref,
    src_out, rel_out, low_out, low_t_out, score_out, gs_out, gr_out, own_out, ghot_out, acc,
):
    chunk = 512
    rel_ids = rid_ref[...]
    acc[...] = jnp.zeros_like(acc)

    def gather(i, carry):
        base = pl.multiple_of(i * chunk, chunk)
        acc[...] += dot(rel_ref[:, pl.ds(base, chunk)], onehot(chunk, rel_ids - base))
        return carry

    lax.fori_loop(0, NREL // chunk, gather, 0)
    rel = acc[...]
    src = dot(own_ref[...], onehot(ENT, src_ref[...]))
    low = complex_product(src, rel).astype(BF16)
    low_t = jnp.transpose(low.astype(F32)).astype(BF16)
    src = src.astype(BF16)
    rel = rel.astype(BF16)
    src_out[...] = src
    rel_out[...] = rel
    low_out[...] = low
    low_t_out[...] = low_t
    hot = hot_ref[...]
    scores = dot(low_t, hot)
    score_out[...] = scores
    mid = slice(EDGES, 2 * EDGES)
    g_source, g_relation, g_far, g_hot = bucket_grads(
        src[:, mid], rel[:, mid], low[:, mid], low_t[mid], own_ref[...], hot, scores[mid],
        dst_ref[:, mid], neg_ref[:, NEG : 2 * NEG], count_ref[1],
    )
    gs_out[...] = g_source
    gr_out[...] = g_relation
    own_out[...] = g_far
    ghot_out[...] = g_hot


def back_kernel(
    next_ref, prev_ref, hot_ref, src_ref, rel_ref, low_ref, low_t_ref, score_ref,
    gs_ref, gr_ref, own_ref, ghot_ref, sid_ref, rid_ref, dst_ref, neg_ref, slot_ref, count_ref, core_ref,
    msg_out, hot_out, own_out, next_out, prev_out,
):
    hot = hot_ref[...]
    sources = [None, gs_ref[...], None]
    relations = [None, gr_ref[...], None]
    g_hot = ghot_ref[...]
    for k, far_ref, far_out in ((0, next_ref, next_out), (2, prev_ref, prev_out)):
        part = slice(k * EDGES, (k + 1) * EDGES)
        g_source, g_relation, g_far, g_hot_k = bucket_grads(
            src_ref[:, part], rel_ref[:, part], low_ref[:, part], low_t_ref[part], far_ref[...],
            hot, score_ref[part], dst_ref[:, part], neg_ref[:, k * NEG : (k + 1) * NEG], count_ref[k],
        )
        sources[k] = g_source
        relations[k] = g_relation
        far_out[...] = g_far.astype(BF16)
        g_hot = g_hot + g_hot_k
    own_out[...] = own_ref[...] + dot_nt(
        jnp.concatenate(sources, axis=1), onehot(ENT, sid_ref[...])
    )
    rel_ids = rid_ref[...]
    place = lax.broadcasted_iota(jnp.int32, (16, LANES), 0)
    for b in range(6):
        ids = rel_ids[:, b * LANES : (b + 1) * LANES]
        high = jnp.right_shift(ids, 6).astype(F32)
        low = jnp.bitwise_and(ids, 63).astype(F32)
        tail = jnp.where(place == 0, high, jnp.where(place == 1, low, 0.0)).astype(BF16)
        piece = relations[b // 2][:, (b % 2) * LANES : (b % 2 + 1) * LANES]
        msg_out[b * REL_ROWS : b * REL_ROWS + D, :] = piece
        msg_out[b * REL_ROWS + D : (b + 1) * REL_ROWS, :] = tail
    slot = slot_ref[...]
    owner = jnp.right_shift(slot, 2)
    spot = (
        jnp.bitwise_and(jnp.right_shift(owner, 1), 1) * 512
        + (jnp.right_shift(owner, 5) * 2 + jnp.bitwise_and(owner, 1)) * 32
        + jnp.bitwise_and(jnp.right_shift(owner, 2), 7) * 4
        + jnp.bitwise_and(slot, 3)
    )
    g_hot = g_hot.astype(BF16)
    core = core_ref[0]
    for base, out, first in ((core * 512, hot_out, 0), ((1 - core) * 512, msg_out, HOT_BASE)):
        rows = dot_nt(onehot(512, spot - base), g_hot).astype(BF16)
        for b in range(HOT_BLOCKS):
            start = first + b * 512
            if b < 3:
                out[start : start + 512, :] = rows[:, b * LANES : (b + 1) * LANES]
            else:
                out[start : start + 512, :] = jnp.concatenate(
                    [rows[:, 3 * LANES :], jnp.zeros((512, HOT_BLOCKS * LANES - D), BF16)], axis=1
                )


def scatter_kernel(mine_ref, got_ref, hot_ref, core_ref, out_ref, grads, id_ref):
    for n, ref in enumerate((mine_ref, got_ref)):
        for b in range(6):
            col = (n * 6 + b) * LANES
            grads[:, col : col + LANES] = ref[b * REL_ROWS : b * REL_ROWS + D, :]
            tail = ref[b * REL_ROWS + D : (b + 1) * REL_ROWS, :].astype(F32)
            ids = tail[0:1] * 64.0 + tail[1:2]
            id_ref[:, col : col + LANES] = ids.astype(jnp.int32)
    first = core_ref[0] * (NREL // 2)

    def step(i, carry):
        hits = onehot(2 * LANES, id_ref[...] - (first + i * 2 * LANES))
        both = dot_nt(grads[...], hits).astype(BF16)
        out_ref[2 * i, :D, :] = both[:, :LANES]
        out_ref[2 * i + 1, :D, :] = both[:, LANES:]
        return carry

    lax.fori_loop(0, PLANE // 2, step, 0)
    for j in range(PLANE):
        for b in range(HOT_BLOCKS):
            row = b * 512 + j * 32
            added = hot_ref[row : row + 32, :].astype(F32) + got_ref[
                HOT_BASE + row : HOT_BASE + row + 32, :
            ].astype(F32)
            out_ref[j, D + b * 32 : D + (b + 1) * 32, :] = added.astype(BF16)


def plane_sum_kernel(in_ref, out_ref):
    total = in_ref[0].astype(F32)
    for j in range(1, PLANE):
        total = total + in_ref[j].astype(F32)
    for z in range(DEPTH):
        low = min(z * Z_REL, D)
        high = min(low + Z_REL, D)
        parts = []
        if high > low:
            parts.append(total[low:high])
        if high - low < Z_REL:
            parts.append(jnp.zeros((Z_REL - (high - low), LANES), F32))
        for b in range(HOT_BLOCKS):
            row = D + b * 32 + z * 4
            parts.append(total[row : row + 4])
        out_ref[z] = jnp.concatenate(parts, axis=0).astype(BF16)


def depth_sum_kernel(in_ref, rel_ref, hot_ref):
    total = in_ref[0].astype(F32)
    for z in range(1, DEPTH):
        total = total + in_ref[z].astype(F32)
    rel = total[:Z_REL].astype(BF16)
    for z in range(DEPTH):
        rel_ref[z] = rel
    for b in range(HOT_BLOCKS):
        width = min(LANES, D - b * LANES)
        hot_ref[:, b * LANES : b * LANES + width] = total[Z_REL + 4 * b : Z_REL + 4 * b + 4, :width]


def merge_kernel(core_ref, mine_ref, got_ref, out_ref):
    same = pl.program_id(0) == core_ref[0]
    for j in range(mine_ref.shape[0]):
        col = j * LANES

        @pl.when(same)
        def _():
            out_ref[:, col : col + LANES] = mine_ref[j].astype(F32)

        @pl.when(jnp.logical_not(same))
        def _():
            out_ref[:, col : col + LANES] = got_ref[j].astype(F32)


def struct(shape, dtype):
    return jax.ShapeDtypeStruct(shape, dtype)


PARAMS = pltpu.CompilerParams(vmem_limit_bytes=48 * 1024 * 1024)
VMEM = pl.BlockSpec(memory_space=pltpu.VMEM)
SMEM = pl.BlockSpec(memory_space=pltpu.SMEM)


def moved(value, axis, count, steps):
    return lax.ppermute(value, axis, [(i, (i + steps) % count) for i in range(count)])


def shards(entities, hot_entities, relations, src_ids, rel_ids, dst_ids, neg_ids, counts, hot_slot):
    blocks = lax.axis_size(BLK)
    own = entities.T
    hot = hot_entities.T
    rel = relations.T
    sid = src_ids.reshape(1, -1)
    rid = rel_ids.reshape(1, -1)
    did = dst_ids.reshape(1, -1)
    nid = neg_ids.reshape(1, -1)
    count = counts.reshape(-1)
    slot = hot_slot.reshape(1, -1)
    core = lax.axis_index("core").astype(jnp.int32).reshape(1)
    after = moved(own, BLK, blocks, -1)
    before = moved(own, BLK, blocks, 1)
    edges = sid.shape[1]
    src, relg, low, low_t, scores, gs, gr, own_grad, ghot = pl.pallas_call(
        front_kernel,
        out_shape=(
            struct((D, edges), BF16), struct((D, edges), BF16), struct((D, edges), BF16),
            struct((edges, D), BF16), struct((edges, HOT), F32),
            struct((D, EDGES), BF16), struct((D, EDGES), BF16), struct((D, ENT), F32),
            struct((D, HOT), F32),
        ),
        in_specs=[VMEM] * 7 + [SMEM],
        out_specs=[VMEM] * 9,
        scratch_shapes=[pltpu.VMEM((D, edges), F32)],
        compiler_params=PARAMS,
        cost_estimate=pl.CostEstimate(flops=5 * 10**9, bytes_accessed=10**7, transcendentals=0),
        name="front",
    )(rel, own, hot, sid, rid, did, nid, count)
    msg, hot_mine, own_grad, next_grad, prev_grad = pl.pallas_call(
        back_kernel,
        out_shape=(
            struct((MSG_ROWS, LANES), BF16), struct((HOT_BLOCKS * 512, LANES), BF16),
            struct((D, ENT), F32), struct((D, ENT), BF16), struct((D, ENT), BF16),
        ),
        in_specs=[VMEM] * 17 + [SMEM] * 2,
        out_specs=[VMEM] * 5,
        compiler_params=PARAMS,
        cost_estimate=pl.CostEstimate(flops=4 * 10**9, bytes_accessed=10**7, transcendentals=0),
        name="back",
    )(after, before, hot, src, relg, low, low_t, scores, gs, gr, own_grad, ghot,
      sid, rid, did, nid, slot, count, core)
    swap = [(0, 1), (1, 0)]
    got = lax.ppermute(msg, "core", swap)
    from_prev = moved(next_grad, BLK, blocks, 1)
    from_next = moved(prev_grad, BLK, blocks, -1)
    slabs = pl.pallas_call(
        scatter_kernel,
        out_shape=struct((PLANE, SLAB, LANES), BF16),
        in_specs=[VMEM] * 3 + [SMEM],
        out_specs=VMEM,
        scratch_shapes=[pltpu.VMEM((D, 2 * edges), BF16), pltpu.VMEM((1, 2 * edges), jnp.int32)],
        compiler_params=PARAMS,
        cost_estimate=pl.CostEstimate(flops=2 * 10**9, bytes_accessed=10**7, transcendentals=0),
        name="spread",
    )(msg, got, hot_mine, core)
    slabs = lax.all_to_all(slabs, YX, 0, 0, tiled=True)
    pieces = pl.pallas_call(
        plane_sum_kernel,
        out_shape=struct((DEPTH, Z_ROWS, LANES), BF16),
        in_specs=[VMEM],
        out_specs=VMEM,
        compiler_params=PARAMS,
        name="plane_sum",
    )(slabs)
    pieces = lax.all_to_all(pieces, "z", 0, 0, tiled=True)
    column, hot_grad = pl.pallas_call(
        depth_sum_kernel,
        out_shape=(struct((DEPTH, Z_REL, LANES), BF16), struct((4, D), F32)),
        in_specs=[VMEM],
        out_specs=(VMEM, VMEM),
        compiler_params=PARAMS,
        name="depth_sum",
    )(pieces)
    column = lax.all_to_all(column, "z", 0, 0, tiled=True)
    column = column.reshape(DEPTH * Z_REL, LANES)[:D]
    mine = lax.all_to_all(
        jnp.broadcast_to(column[None], (PLANE, D, LANES)), YX, 0, 0, tiled=True
    )
    other = lax.ppermute(mine, "core", swap)
    group = 4
    relation_grad = pl.pallas_call(
        merge_kernel,
        out_shape=struct((D, NREL), F32),
        grid_spec=pltpu.PrefetchScalarGridSpec(
            num_scalar_prefetch=1,
            grid=(2, PLANE // group),
            in_specs=[
                pl.BlockSpec((group, D, LANES), lambda h, i, c: (i, 0, 0)),
                pl.BlockSpec((group, D, LANES), lambda h, i, c: (i, 0, 0)),
            ],
            out_specs=pl.BlockSpec((D, group * LANES), lambda h, i, c: (0, h * (PLANE // group) + i)),
        ),
        compiler_params=PARAMS,
        name="merge",
    )(core, mine, other)
    part = (own_grad + from_prev.astype(F32) + from_next.astype(F32)).astype(BF16)
    twin = lax.ppermute(part, "rep", swap)
    entity_grad = part.astype(F32) + twin.astype(F32)
    return entity_grad.T, relation_grad.T, hot_grad


def solution(mesh):
    inner = Mesh(mesh.devices.reshape(4, 2, 8, 2, 2), ("y", "xh", "z", "core", "rep"))
    return jax.shard_map(
        shards,
        mesh=inner,
        in_specs=(
            P(BLK, None),
            P(),
            P(),
            P(BLK, "rep", None, None),
            P(BLK, "rep", None, None),
            P(BLK, "rep", None, None),
            P(BLK, "rep", None, None),
            P(BLK, "rep", None),
            P(),
        ),
        out_specs=(P(BLK, None), P(), P(BLK + ("rep",), None)),
        check_vma=False,
    )
```

```python
import functools
import jax
import jax.numpy as jnp
import numpy as np
from jax import lax
from jax.experimental import pallas as pl
from jax.experimental.pallas import tpu as pltpu
from jax.sharding import Mesh, PartitionSpec as P

F32 = jnp.float32
BF16 = jnp.bfloat16
D = 400
HALF_D = 200
NREL = 4096
EDGES = 256
NEG = 512
ENT = 512
HOT = 1024
GROUP = 32
QUAD = 4
LANES = 128
REL_ROWS = D + 16
HOT_BASE = 6 * REL_ROWS
HOT_BLOCKS = 4
MSG_ROWS = HOT_BASE + HOT_BLOCKS * 512
TAIL = HALF_D
HOT_AT = HALF_D + 8
SLAB = HOT_AT + 3 * 16
PIECE = 224
PARTS = 4
SPREAD = 512
BLK = ("y", "xh", "zh", "zl", "core")
NEAR = ("y", "xh", "zl", "rep")


def onehot(rows, ids):
    grid = lax.broadcasted_iota(jnp.int32, (rows, ids.shape[1]), 0)
    return jnp.where(grid == ids, 1.0, 0.0).astype(BF16)


def dot(a, b):
    return lax.dot_general(a, b, (((1,), (0,)), ((), ())), preferred_element_type=F32)


def dot_nt(a, b):
    return lax.dot_general(a, b, (((1,), (1,)), ((), ())), preferred_element_type=F32)


def to_column(row):
    return jnp.transpose(jnp.broadcast_to(row, (8, row.shape[1])))[:, :1]


def to_row(column):
    return jnp.transpose(jnp.broadcast_to(column, (column.shape[0], LANES)))[:1]


def halves(value):
    return value[:HALF_D], value[HALF_D:]


def complex_product(left, right):
    lr, li = halves(left)
    rr, ri = halves(right)
    return jnp.concatenate([lr * rr - li * ri, lr * ri + li * rr], axis=0)


def conj_product(left, right):
    lr, li = halves(left)
    rr, ri = halves(right)
    return jnp.concatenate([lr * rr + li * ri, li * rr - lr * ri], axis=0)


def bucket_grads(src, rel, low, low_t, far, hot, hot_scores, dst, neg, count):
    src = src.astype(F32)
    rel = rel.astype(F32)
    product = complex_product(src, rel)
    dst_hot = onehot(ENT, dst)
    target = dot(far, dst_hot)
    positive = to_column(jnp.sum(product * target, axis=0, keepdims=True))
    table = dot_nt(
        onehot(16, jnp.right_shift(neg, 7)), onehot(LANES, jnp.bitwise_and(neg, LANES - 1))
    )
    times = jnp.concatenate(
        [table[i : i + 1] for i in range((ENT + HOT) // LANES)], axis=1
    )
    bias = jnp.where(times > 0.0, jnp.log(jnp.maximum(times, 1.0)), -1e30)
    score_far = dot(low_t, far) + bias[:, :ENT]
    score_hot = hot_scores + bias[:, ENT:]
    peak = jnp.maximum(
        jnp.max(score_far, axis=1, keepdims=True), jnp.max(score_hot, axis=1, keepdims=True)
    )
    peak = jnp.maximum(peak, positive)
    exp_far = jnp.exp(score_far - peak)
    exp_hot = jnp.exp(score_hot - peak)
    exp_positive = jnp.exp(positive - peak)
    total = (
        exp_positive
        + jnp.sum(exp_far, axis=1, keepdims=True)
        + jnp.sum(exp_hot, axis=1, keepdims=True)
    )
    live = jnp.where(lax.broadcasted_iota(jnp.int32, (EDGES, 1), 0) < count, 1.0, 0.0)
    g_positive = to_row(live * (exp_positive / total - 1.0))
    scale = live / total
    w_far = (exp_far * scale).astype(BF16)
    w_hot = (exp_hot * scale).astype(BF16)
    g_product = g_positive * target + dot_nt(far, w_far) + dot_nt(hot, w_hot)
    g_source = conj_product(g_product, rel).astype(BF16)
    g_relation = conj_product(g_product, src).astype(BF16)
    g_target = (g_positive * product).astype(BF16)
    g_hot = dot(low, w_hot)
    return g_source, g_relation, g_target, w_far, g_hot


def lookup_kernel(rel_hbm, rid_ref, rel_out, acc, rel_ref, sems):
    chunk = NREL // PARTS
    copies = []
    for i in range(PARTS):
        part = pl.ds(i * chunk, chunk)
        copies.append(
            pltpu.make_async_copy(rel_hbm.at[:, part], rel_ref.at[:, part], sems.at[i])
        )
    for copy in copies:
        copy.start()
    rel_ids = rid_ref[...]
    for i in range(PARTS):
        base = i * chunk
        hits = onehot(chunk, rel_ids - base)
        copies[i].wait()
        found = dot(rel_ref[:, base : base + chunk], hits)
        if i == 0:
            acc[...] = found
        elif i < PARTS - 1:
            acc[...] += found
        else:
            rel_out[...] = (acc[...] + found).astype(BF16)


def front_kernel(
    rel_ref, own_ref, hot_ref, src_ref, dst_ref, neg_ref, count_ref,
    src_out, low_out, low_t_out, score_out, gs_out, gr_out, gt_out, wf_out, ghot_out,
):
    rel = rel_ref[...]
    src = dot(own_ref[...], onehot(ENT, src_ref[...]))
    low = complex_product(src, rel.astype(F32)).astype(BF16)
    low_t = jnp.transpose(low.astype(F32)).astype(BF16)
    src = src.astype(BF16)
    src_out[...] = src
    low_out[...] = low
    low_t_out[...] = low_t
    hot = hot_ref[...]
    scores = dot(low_t, hot)
    score_out[...] = scores
    mid = slice(EDGES, 2 * EDGES)
    g_source, g_relation, g_target, w_far, g_hot = bucket_grads(
        src[:, mid], rel[:, mid], low[:, mid], low_t[mid], own_ref[...], hot, scores[mid],
        dst_ref[:, mid], neg_ref[:, NEG : 2 * NEG], count_ref[1],
    )
    gs_out[...] = g_source
    gr_out[...] = g_relation
    gt_out[...] = g_target
    wf_out[...] = w_far
    ghot_out[...] = g_hot


def back_kernel(
    next_ref, prev_ref, hot_ref, src_ref, rel_ref, low_ref, low_t_ref, score_ref,
    gr_ref, ghot_ref, rid_ref, dst_ref, neg_ref, slot_ref, count_ref, core_ref,
    msg_out, all_out, hot_out, gs0_out, gs2_out, gt0_out, gt2_out, wf0_out, wf2_out,
):
    hot = hot_ref[...]
    relations = [None, gr_ref[...], None]
    g_hot = ghot_ref[...]
    for k, far_ref, gs_out, gt_out, wf_out in (
        (0, next_ref, gs0_out, gt0_out, wf0_out),
        (2, prev_ref, gs2_out, gt2_out, wf2_out),
    ):
        part = slice(k * EDGES, (k + 1) * EDGES)
        g_source, g_relation, g_target, w_far, g_hot_k = bucket_grads(
            src_ref[:, part], rel_ref[:, part], low_ref[:, part], low_t_ref[part], far_ref[...],
            hot, score_ref[part], dst_ref[:, part], neg_ref[:, k * NEG : (k + 1) * NEG], count_ref[k],
        )
        relations[k] = g_relation
        gs_out[...] = g_source
        gt_out[...] = g_target
        wf_out[...] = w_far
        g_hot = g_hot + g_hot_k
    rel_ids = rid_ref[...]
    place = lax.broadcasted_iota(jnp.int32, (16, LANES), 0)
    for b in range(6):
        ids = rel_ids[:, b * LANES : (b + 1) * LANES]
        high = jnp.right_shift(ids, 6).astype(F32)
        low = jnp.bitwise_and(ids, 63).astype(F32)
        tail = jnp.where(place == 0, high, jnp.where(place == 1, low, 0.0)).astype(BF16)
        piece = relations[b // 2][:, (b % 2) * LANES : (b % 2 + 1) * LANES]
        msg_out[b * REL_ROWS : b * REL_ROWS + D, :] = piece
        all_out[:, b * LANES : (b + 1) * LANES] = piece
        msg_out[b * REL_ROWS + D : (b + 1) * REL_ROWS, :] = tail
    slot = slot_ref[...]
    owner = jnp.right_shift(slot, 2)
    spot = (
        jnp.bitwise_and(jnp.right_shift(owner, 1), 1) * 512
        + jnp.right_shift(owner, 5) * 64
        + jnp.bitwise_and(jnp.right_shift(owner, 2), 1) * 32
        + jnp.bitwise_and(owner, 1) * 16
        + jnp.bitwise_and(jnp.right_shift(owner, 3), 3) * 4
        + jnp.bitwise_and(slot, 3)
    )
    g_hot = g_hot.astype(BF16)
    core = core_ref[0]
    for base, out, first in ((core * 512, hot_out, 0), ((1 - core) * 512, msg_out, HOT_BASE)):
        rows = dot_nt(onehot(512, spot - base), g_hot).astype(BF16)
        for b in range(HOT_BLOCKS):
            start = first + b * 512
            if b < 3:
                out[start : start + 512, :] = rows[:, b * LANES : (b + 1) * LANES]
            else:
                out[start : start + 512, :] = jnp.concatenate(
                    [rows[:, 3 * LANES :], jnp.zeros((512, HOT_BLOCKS * LANES - D), BF16)], axis=1
                )


def tail_kernel(
    low_ref, gs0_ref, gs1_ref, gs2_ref, gt0_ref, gt1_ref, gt2_ref, wf0_ref, wf1_ref, wf2_ref,
    sid_ref, dst_ref, own_out, next_out, prev_out,
):
    ids = sid_ref[...]
    own = None
    for k, gs_ref, gt_ref, wf_ref, far_out in (
        (0, gs0_ref, gt0_ref, wf0_ref, next_out),
        (2, gs2_ref, gt2_ref, wf2_ref, prev_out),
        (1, gs1_ref, gt1_ref, wf1_ref, None),
    ):
        part = slice(k * EDGES, (k + 1) * EDGES)
        far = dot(low_ref[:, part], wf_ref[...]) + dot_nt(gt_ref[...], onehot(ENT, dst_ref[:, part]))
        near = dot_nt(gs_ref[...], onehot(ENT, ids[:, part]))
        own = near if own is None else own + near
        if far_out is None:
            own = own + far
        else:
            far_out[...] = far.astype(BF16)
    own_out[...] = own


def spread_kernel(grad_ref, rid_ref, got_ref, hot_ref, core_ref, out_ref, grads, id_ref, slabs, sems):
    edges = grad_ref.shape[1]
    grads[:, :edges] = grad_ref[...]
    id_ref[:, :edges] = rid_ref[...]
    for b in range(6):
        col = edges + b * LANES
        grads[:, col : col + LANES] = got_ref[b * REL_ROWS : b * REL_ROWS + D, :]
        tail = got_ref[b * REL_ROWS + D : (b + 1) * REL_ROWS, :].astype(F32)
        ids = tail[0:1] * 64.0 + tail[1:2]
        id_ref[:, col : col + LANES] = ids.astype(jnp.int32)
    ids = id_ref[...] - core_ref[0] * (NREL // 2)
    copies = []
    for i in range(NREL // 2 // SPREAD):
        wide = dot_nt(grads[...], onehot(SPREAD, ids - i * SPREAD))
        count = SPREAD // LANES
        for n in range(count):
            for zl in range(2):
                j = 2 * count * i + 4 * (n // 2) + 2 * zl + n % 2
                hot = []
                for b in range(HOT_BLOCKS):
                    row = b * 512 + j * 16
                    hot.append(
                        hot_ref[row : row + 16, :].astype(F32)
                        + got_ref[HOT_BASE + row : HOT_BASE + row + 16, :].astype(F32)
                    )
                last = hot.pop()
                tail = jnp.concatenate(
                    [last[:8, :16], last[8:, :16], jnp.zeros((8, LANES - 32), F32)], axis=1
                )
                piece = wide[zl * HALF_D : (zl + 1) * HALF_D, n * LANES : (n + 1) * LANES]
                slabs[j] = jnp.concatenate([piece, tail] + hot, axis=0).astype(BF16)
        part = pl.ds(2 * count * i, 2 * count)
        copy = pltpu.make_async_copy(slabs.at[part], out_ref.at[part], sems.at[i])
        copy.start()
        copies.append(copy)
    for copy in copies:
        copy.wait()


def near_sum_kernel(in_ref, out_ref):
    total = in_ref[0].astype(F32)
    for j in range(1, GROUP):
        total = total + in_ref[j].astype(F32)
    for zh in range(QUAD):
        parts = [total[:HALF_D]]
        for b in range(3):
            row = HOT_AT + b * 16 + zh * 4
            parts.append(total[row : row + 4])
        row, col = TAIL + (zh % 2) * 4, (zh // 2) * 16
        parts.append(
            jnp.concatenate(
                [total[row : row + 4, col : col + 16], jnp.zeros((4, LANES - 16), F32)], axis=1
            )
        )
        parts.append(jnp.zeros((PIECE - HALF_D - 16, LANES), F32))
        out_ref[zh] = jnp.concatenate(parts, axis=0).astype(BF16)


def quad_sum_kernel(in_ref, rel_ref, hot_ref):
    total = in_ref[0].astype(F32)
    for zh in range(1, QUAD):
        total = total + in_ref[zh].astype(F32)
    rel = total[:HALF_D].astype(BF16)
    for j in range(GROUP):
        rel_ref[j] = rel
    for b in range(HOT_BLOCKS):
        width = min(LANES, D - b * LANES)
        row = HALF_D + 4 * b
        hot_ref[:, b * LANES : b * LANES + width] = total[row : row + 4, :width]


def merge_kernel(core_ref, in_ref, *refs):
    out_ref = refs[-1]
    for near in range(2):
        for zl in range(2):
            for rep in range(2):
                col = (2 * near + rep) * LANES
                out_ref[zl * HALF_D : (zl + 1) * HALF_D, col : col + LANES] = in_ref[
                    4 * near + 2 * zl + rep
                ].astype(F32)


def merged(core, value, before):
    steps = GROUP // 8
    first = before is None
    if first:
        place = lambda i, c: (0, c[0] * steps + i)
    else:
        place = lambda i, c: (0, (1 - c[0]) * steps + i)
    in_specs = [pl.BlockSpec((8, HALF_D, LANES), lambda i, c: (i, 0, 0))]
    if not first:
        in_specs.append(pl.BlockSpec(memory_space=pl.ANY))
    return pl.pallas_call(
        merge_kernel,
        out_shape=struct((D, NREL), F32),
        grid_spec=pltpu.PrefetchScalarGridSpec(
            num_scalar_prefetch=1,
            grid=(steps,),
            in_specs=in_specs,
            out_specs=pl.BlockSpec((D, 4 * LANES), place),
        ),
        input_output_aliases={} if first else {2: 0},
        compiler_params=PARAMS,
        cost_estimate=pl.CostEstimate(flops=0, bytes_accessed=10**7, transcendentals=0),
        name="merge",
    )(core, value, *([] if first else [before]))


def struct(shape, dtype):
    return jax.ShapeDtypeStruct(shape, dtype)


PARAMS = pltpu.CompilerParams(vmem_limit_bytes=48 * 1024 * 1024)
VMEM = pl.BlockSpec(memory_space=pltpu.VMEM)
SMEM = pl.BlockSpec(memory_space=pltpu.SMEM)
HBM = pl.BlockSpec(memory_space=pltpu.HBM)


def moved(value, axis, count, steps):
    return lax.ppermute(value, axis, [(i, (i + steps) % count) for i in range(count)])


def shards(entities, hot_entities, relations, src_ids, rel_ids, dst_ids, neg_ids, counts, hot_slot):
    blocks = lax.axis_size(BLK)
    own = entities.T
    hot = hot_entities.T
    rel = relations.T
    sid = src_ids.reshape(1, -1)
    rid = rel_ids.reshape(1, -1)
    did = dst_ids.reshape(1, -1)
    nid = neg_ids.reshape(1, -1)
    count = counts.reshape(-1)
    slot = hot_slot.reshape(1, -1)
    core = lax.axis_index("core").astype(jnp.int32).reshape(1)
    after = moved(own, BLK, blocks, -1)
    before = moved(own, BLK, blocks, 1)
    edges = sid.shape[1]
    relg = pl.pallas_call(
        lookup_kernel,
        out_shape=struct((D, edges), BF16),
        in_specs=[HBM, VMEM],
        out_specs=VMEM,
        scratch_shapes=[
            pltpu.VMEM((D, edges), F32),
            pltpu.VMEM((D, NREL), BF16),
            pltpu.SemaphoreType.DMA((PARTS,)),
        ],
        compiler_params=PARAMS,
        cost_estimate=pl.CostEstimate(flops=3 * 10**9, bytes_accessed=10**7, transcendentals=0),
        name="lookup",
    )(rel, rid)
    half = struct((D, EDGES), BF16)
    weight = struct((EDGES, ENT), BF16)
    src, low, low_t, scores, gs1, gr, gt1, wf1, ghot = pl.pallas_call(
        front_kernel,
        out_shape=(
            struct((D, edges), BF16), struct((D, edges), BF16),
            struct((edges, D), BF16), struct((edges, HOT), F32),
            half, half, half, weight, struct((D, HOT), F32),
        ),
        in_specs=[VMEM] * 6 + [SMEM],
        out_specs=[VMEM] * 9,
        compiler_params=PARAMS,
        cost_estimate=pl.CostEstimate(flops=5 * 10**9, bytes_accessed=10**7, transcendentals=0),
        name="front",
    )(relg, own, hot, sid, did, nid, count)
    msg, grads, hot_mine, gs0, gs2, gt0, gt2, wf0, wf2 = pl.pallas_call(
        back_kernel,
        out_shape=(
            struct((MSG_ROWS, LANES), BF16), struct((D, edges), BF16),
            struct((HOT_BLOCKS * 512, LANES), BF16),
            half, half, half, half, weight, weight,
        ),
        in_specs=[VMEM] * 14 + [SMEM] * 2,
        out_specs=[VMEM] * 9,
        compiler_params=PARAMS,
        cost_estimate=pl.CostEstimate(flops=4 * 10**9, bytes_accessed=10**7, transcendentals=0),
        name="back",
    )(after, before, hot, src, relg, low, low_t, scores, gr, ghot,
      rid, did, nid, slot, count, core)
    own_grad, next_grad, prev_grad = pl.pallas_call(
        tail_kernel,
        out_shape=(struct((D, ENT), F32), struct((D, ENT), BF16), struct((D, ENT), BF16)),
        in_specs=[VMEM] * 12,
        out_specs=[VMEM] * 3,
        compiler_params=PARAMS,
        cost_estimate=pl.CostEstimate(flops=4 * 10**9, bytes_accessed=10**7, transcendentals=0),
        name="tail",
    )(low, gs0, gs1, gs2, gt0, gt1, gt2, wf0, wf1, wf2, sid, did)
    swap = [(0, 1), (1, 0)]
    got = lax.ppermute(msg, "core", swap)
    from_prev = moved(next_grad, BLK, blocks, 1)
    from_next = moved(prev_grad, BLK, blocks, -1)
    slabs = pl.pallas_call(
        spread_kernel,
        out_shape=struct((GROUP, SLAB, LANES), BF16),
        in_specs=[VMEM] * 4 + [SMEM],
        out_specs=HBM,
        scratch_shapes=[
            pltpu.VMEM((D, 2 * edges), BF16),
            pltpu.VMEM((1, 2 * edges), jnp.int32),
            pltpu.VMEM((GROUP, SLAB, LANES), BF16),
            pltpu.SemaphoreType.DMA((NREL // 2 // SPREAD,)),
        ],
        compiler_params=PARAMS,
        cost_estimate=pl.CostEstimate(flops=10**9, bytes_accessed=10**7, transcendentals=0),
        name="spread",
    )(grads, rid, got, hot_mine, core)
    slabs = lax.all_to_all(slabs, NEAR, 0, 0, tiled=True)
    part = (own_grad + from_prev.astype(F32) + from_next.astype(F32)).astype(BF16)
    slabs, part = lax.optimization_barrier((slabs, part))
    twin = lax.ppermute(part, "rep", swap)
    pieces = pl.pallas_call(
        near_sum_kernel,
        out_shape=struct((QUAD, PIECE, LANES), BF16),
        in_specs=[VMEM],
        out_specs=VMEM,
        compiler_params=PARAMS,
        name="near_sum",
    )(slabs)
    pieces = lax.all_to_all(pieces, "zh", 0, 0, tiled=True)
    pieces, twin = lax.optimization_barrier((pieces, twin))
    column, hot_grad = pl.pallas_call(
        quad_sum_kernel,
        out_shape=(struct((GROUP, HALF_D, LANES), BF16), struct((4, D), F32)),
        in_specs=[VMEM],
        out_specs=(VMEM, VMEM),
        compiler_params=PARAMS,
        name="quad_sum",
    )(pieces)
    mine = lax.all_to_all(column, NEAR, 0, 0, tiled=True)
    other = lax.ppermute(mine, "core", swap)
    relation_grad = merged(core, other, merged(core, mine, None))
    entity_grad = part.astype(F32) + twin.astype(F32)
    return entity_grad.T, relation_grad.T, hot_grad


def solution(mesh):
    inner = Mesh(mesh.devices.reshape(4, 2, 4, 2, 2, 2), BLK + ("rep",))
    return jax.shard_map(
        shards,
        mesh=inner,
        in_specs=(
            P(BLK, None),
            P(),
            P(),
            P(BLK, "rep", None, None),
            P(BLK, "rep", None, None),
            P(BLK, "rep", None, None),
            P(BLK, "rep", None, None),
            P(BLK, "rep", None),
            P(),
        ),
        out_specs=(P(BLK, None), P(), P(BLK + ("rep",), None)),
        check_vma=False,
    )
```

```python
import functools
import jax
import jax.numpy as jnp
import numpy as np
from jax import lax
from jax.experimental import pallas as pl
from jax.experimental.pallas import tpu as pltpu
from jax.sharding import Mesh, PartitionSpec as P

F32 = jnp.float32
BF16 = jnp.bfloat16
D = 400
HALF_D = 200
NREL = 4096
EDGES = 256
NEG = 512
ENT = 512
HOT = 1024
GROUP = 32
QUAD = 4
LANES = 128
REL_ROWS = D + 16
HOT_BASE = 6 * REL_ROWS
HOT_BLOCKS = 4
MSG_ROWS = HOT_BASE + HOT_BLOCKS * 512
TAIL = HALF_D
HOT_AT = HALF_D + 8
SLAB = HOT_AT + 3 * 16
PIECE = 224
WIDE = 256
SPREAD = 512
BLK = ("y", "xh", "zh", "zl", "core")
NEAR = ("y", "xh", "zl", "rep")


def onehot(rows, ids):
    grid = lax.broadcasted_iota(jnp.int32, (rows, ids.shape[1]), 0)
    return jnp.where(grid == ids, 1.0, 0.0).astype(BF16)


def dot(a, b):
    return lax.dot_general(a, b, (((1,), (0,)), ((), ())), preferred_element_type=F32)


def dot_nt(a, b):
    return lax.dot_general(a, b, (((1,), (1,)), ((), ())), preferred_element_type=F32)


def to_column(row):
    return jnp.transpose(jnp.broadcast_to(row, (8, row.shape[1])))[:, :1]


def to_row(column):
    return jnp.transpose(jnp.broadcast_to(column, (column.shape[0], LANES)))[:1]


def halves(value):
    return value[:HALF_D], value[HALF_D:]


def complex_product(left, right):
    lr, li = halves(left)
    rr, ri = halves(right)
    return jnp.concatenate([lr * rr - li * ri, lr * ri + li * rr], axis=0)


def conj_product(left, right):
    lr, li = halves(left)
    rr, ri = halves(right)
    return jnp.concatenate([lr * rr + li * ri, li * rr - lr * ri], axis=0)


def bucket_grads(src, rel, low, low_t, far, hot, dst, neg, count):
    src = src.astype(F32)
    rel = rel.astype(F32)
    product = complex_product(src, rel)
    dst_hot = onehot(ENT, dst)
    target = dot(far, dst_hot)
    positive = to_column(jnp.sum(product * target, axis=0, keepdims=True))
    table = dot_nt(
        onehot(16, jnp.right_shift(neg, 7)), onehot(LANES, jnp.bitwise_and(neg, LANES - 1))
    )
    times = jnp.concatenate(
        [table[i : i + 1] for i in range((ENT + HOT) // LANES)], axis=1
    )
    bias = jnp.where(times > 0.0, jnp.log(jnp.maximum(times, 1.0)), -1e30)
    score_far = dot(low_t, far) + bias[:, :ENT]
    score_hot = dot(low_t, hot) + bias[:, ENT:]
    peak = jnp.maximum(
        jnp.max(score_far, axis=1, keepdims=True), jnp.max(score_hot, axis=1, keepdims=True)
    )
    peak = jnp.maximum(peak, positive)
    exp_far = jnp.exp(score_far - peak)
    exp_hot = jnp.exp(score_hot - peak)
    exp_positive = jnp.exp(positive - peak)
    total = (
        exp_positive
        + jnp.sum(exp_far, axis=1, keepdims=True)
        + jnp.sum(exp_hot, axis=1, keepdims=True)
    )
    live = jnp.where(lax.broadcasted_iota(jnp.int32, (EDGES, 1), 0) < count, 1.0, 0.0)
    g_positive = to_row(live * (exp_positive / total - 1.0))
    scale = live / total
    w_far = (exp_far * scale).astype(BF16)
    w_hot = (exp_hot * scale).astype(BF16)
    g_product = g_positive * target + dot_nt(far, w_far) + dot_nt(hot, w_hot)
    g_source = conj_product(g_product, rel).astype(BF16)
    g_relation = conj_product(g_product, src).astype(BF16)
    g_target = (g_positive * product).astype(BF16)
    g_far = dot(low, w_far) + dot_nt(g_target, dst_hot)
    return g_source, g_relation, g_far, w_hot


def lookup_kernel(rel_ref, rid_ref, out_ref):
    for start in range(0, rid_ref.shape[1], WIDE):
        part = slice(start, start + WIDE)
        out_ref[:, part] = dot(rel_ref[...], onehot(NREL, rid_ref[:, part])).astype(BF16)


def front_kernel(
    rel_ref, own_ref, hot_ref, src_ref, dst_ref, neg_ref, count_ref,
    src_out, low_out, low_t_out, gr_out, own_out, wh_out,
):
    rel = rel_ref[...]
    places = onehot(ENT, src_ref[...])
    src = dot(own_ref[...], places)
    low = complex_product(src, rel.astype(F32)).astype(BF16)
    low_t = jnp.transpose(low.astype(F32)).astype(BF16)
    src = src.astype(BF16)
    src_out[...] = src
    low_out[...] = low
    low_t_out[...] = low_t
    hot = hot_ref[...]
    mid = slice(EDGES, 2 * EDGES)
    g_source, g_relation, g_far, w_hot = bucket_grads(
        src[:, mid], rel[:, mid], low[:, mid], low_t[mid], own_ref[...], hot,
        dst_ref[:, mid], neg_ref[:, NEG : 2 * NEG], count_ref[1],
    )
    gr_out[...] = g_relation
    own_out[...] = g_far + dot_nt(g_source, places[:, mid])
    wh_out[...] = w_hot


def back_kernel(
    k, far_ref, hot_ref, src_ref, rel_ref, low_ref, low_t_ref, dst_ref, neg_ref, count_ref,
    gs_out, gr_out, wh_out, far_out,
):
    part = slice(k * EDGES, (k + 1) * EDGES)
    g_source, g_relation, g_far, w_hot = bucket_grads(
        src_ref[:, part], rel_ref[:, part], low_ref[:, part], low_t_ref[part], far_ref[...],
        hot_ref[...], dst_ref[:, part], neg_ref[:, k * NEG : (k + 1) * NEG], count_ref[k],
    )
    gs_out[...] = g_source
    gr_out[...] = g_relation
    wh_out[...] = w_hot
    far_out[...] = g_far.astype(BF16)


def pack_kernel(
    gr0_ref, gr1_ref, gr2_ref, wh0_ref, wh1_ref, wh2_ref, low_ref, rid_ref, slot_ref, core_ref,
    msg_out, all_out, hot_out,
):
    relations = [gr0_ref[...], gr1_ref[...], gr2_ref[...]]
    weights = [wh0_ref[...], wh1_ref[...], wh2_ref[...]]
    rel_ids = rid_ref[...]
    place = lax.broadcasted_iota(jnp.int32, (16, LANES), 0)
    for b in range(6):
        ids = rel_ids[:, b * LANES : (b + 1) * LANES]
        high = jnp.right_shift(ids, 6).astype(F32)
        low = jnp.bitwise_and(ids, 63).astype(F32)
        tail = jnp.where(place == 0, high, jnp.where(place == 1, low, 0.0)).astype(BF16)
        piece = relations[b // 2][:, (b % 2) * LANES : (b % 2 + 1) * LANES]
        msg_out[b * REL_ROWS : b * REL_ROWS + D, :] = piece
        all_out[:, b * LANES : (b + 1) * LANES] = piece
        msg_out[b * REL_ROWS + D : (b + 1) * REL_ROWS, :] = tail
    slot = slot_ref[...]
    owner = jnp.right_shift(slot, 2)
    spot = (
        jnp.bitwise_and(jnp.right_shift(owner, 1), 1) * 512
        + jnp.right_shift(owner, 5) * 64
        + jnp.bitwise_and(jnp.right_shift(owner, 2), 1) * 32
        + jnp.bitwise_and(owner, 1) * 16
        + jnp.bitwise_and(jnp.right_shift(owner, 3), 3) * 4
        + jnp.bitwise_and(slot, 3)
    )
    g_hot = dot(low_ref[...], jnp.concatenate(weights, axis=0)).astype(BF16)
    core = core_ref[0]
    for base, out, first in ((core * 512, hot_out, 0), ((1 - core) * 512, msg_out, HOT_BASE)):
        rows = dot_nt(onehot(512, spot - base), g_hot).astype(BF16)
        for b in range(HOT_BLOCKS):
            start = first + b * 512
            if b < 3:
                out[start : start + 512, :] = rows[:, b * LANES : (b + 1) * LANES]
            else:
                out[start : start + 512, :] = jnp.concatenate(
                    [rows[:, 3 * LANES :], jnp.zeros((512, HOT_BLOCKS * LANES - D), BF16)], axis=1
                )


def tail_kernel(own_ref, gs0_ref, gs2_ref, sid_ref, own_out):
    ids = sid_ref[...]
    total = own_ref[...]
    for k, gs_ref in ((0, gs0_ref), (2, gs2_ref)):
        total = total + dot_nt(gs_ref[...], onehot(ENT, ids[:, k * EDGES : (k + 1) * EDGES]))
    own_out[...] = total


def spread_kernel(grad_ref, rid_ref, got_ref, hot_ref, core_ref, out_ref, grads, id_ref, slabs, sems):
    edges = grad_ref.shape[1]
    grads[:, :edges] = grad_ref[...]
    id_ref[:, :edges] = rid_ref[...]
    for b in range(6):
        col = edges + b * LANES
        grads[:, col : col + LANES] = got_ref[b * REL_ROWS : b * REL_ROWS + D, :]
        tail = got_ref[b * REL_ROWS + D : (b + 1) * REL_ROWS, :].astype(F32)
        ids = tail[0:1] * 64.0 + tail[1:2]
        id_ref[:, col : col + LANES] = ids.astype(jnp.int32)
    ids = id_ref[...] - core_ref[0] * (NREL // 2)
    copies = []
    for i in range(NREL // 2 // SPREAD):
        wide = dot_nt(grads[...], onehot(SPREAD, ids - i * SPREAD))
        count = SPREAD // LANES
        for n in range(count):
            for zl in range(2):
                j = 2 * count * i + 4 * (n // 2) + 2 * zl + n % 2
                hot = []
                for b in range(HOT_BLOCKS):
                    row = b * 512 + j * 16
                    hot.append(
                        hot_ref[row : row + 16, :].astype(F32)
                        + got_ref[HOT_BASE + row : HOT_BASE + row + 16, :].astype(F32)
                    )
                last = hot.pop()
                tail = jnp.concatenate(
                    [last[:8, :16], last[8:, :16], jnp.zeros((8, LANES - 32), F32)], axis=1
                )
                piece = wide[zl * HALF_D : (zl + 1) * HALF_D, n * LANES : (n + 1) * LANES]
                slabs[j] = jnp.concatenate([piece, tail] + hot, axis=0).astype(BF16)
        part = pl.ds(2 * count * i, 2 * count)
        copy = pltpu.make_async_copy(slabs.at[part], out_ref.at[part], sems.at[i])
        copy.start()
        copies.append(copy)
    for copy in copies:
        copy.wait()


def near_sum_kernel(in_ref, out_ref):
    total = in_ref[0].astype(F32)
    for j in range(1, GROUP):
        total = total + in_ref[j].astype(F32)
    for zh in range(QUAD):
        parts = [total[:HALF_D]]
        for b in range(3):
            row = HOT_AT + b * 16 + zh * 4
            parts.append(total[row : row + 4])
        row, col = TAIL + (zh % 2) * 4, (zh // 2) * 16
        parts.append(
            jnp.concatenate(
                [total[row : row + 4, col : col + 16], jnp.zeros((4, LANES - 16), F32)], axis=1
            )
        )
        parts.append(jnp.zeros((PIECE - HALF_D - 16, LANES), F32))
        out_ref[zh] = jnp.concatenate(parts, axis=0).astype(BF16)


def quad_sum_kernel(in_ref, rel_ref, hot_ref):
    total = in_ref[0].astype(F32)
    for zh in range(1, QUAD):
        total = total + in_ref[zh].astype(F32)
    rel = total[:HALF_D].astype(BF16)
    for j in range(GROUP):
        rel_ref[j] = rel
    for b in range(HOT_BLOCKS):
        width = min(LANES, D - b * LANES)
        row = HALF_D + 4 * b
        hot_ref[:, b * LANES : b * LANES + width] = total[row : row + 4, :width]


def merge_kernel(core_ref, in_ref, *refs):
    out_ref = refs[-1]
    for near in range(2):
        for zl in range(2):
            for rep in range(2):
                col = (2 * near + rep) * LANES
                out_ref[zl * HALF_D : (zl + 1) * HALF_D, col : col + LANES] = in_ref[
                    4 * near + 2 * zl + rep
                ].astype(F32)


def merged(core, value, before):
    steps = GROUP // 8
    first = before is None
    if first:
        place = lambda i, c: (0, c[0] * steps + i)
    else:
        place = lambda i, c: (0, (1 - c[0]) * steps + i)
    in_specs = [pl.BlockSpec((8, HALF_D, LANES), lambda i, c: (i, 0, 0))]
    if not first:
        in_specs.append(pl.BlockSpec(memory_space=pl.ANY))
    return pl.pallas_call(
        merge_kernel,
        out_shape=struct((D, NREL), F32),
        grid_spec=pltpu.PrefetchScalarGridSpec(
            num_scalar_prefetch=1,
            grid=(steps,),
            in_specs=in_specs,
            out_specs=pl.BlockSpec((D, 4 * LANES), place),
        ),
        input_output_aliases={} if first else {2: 0},
        compiler_params=PARAMS,
        cost_estimate=pl.CostEstimate(flops=0, bytes_accessed=10**7, transcendentals=0),
        name="merge",
    )(core, value, *([] if first else [before]))


def struct(shape, dtype):
    return jax.ShapeDtypeStruct(shape, dtype)


COST = pl.CostEstimate(flops=10**8, bytes_accessed=10**6, transcendentals=0)
PARAMS = pltpu.CompilerParams(vmem_limit_bytes=28 * 1024 * 1024)
VMEM = pl.BlockSpec(memory_space=pltpu.VMEM)
SMEM = pl.BlockSpec(memory_space=pltpu.SMEM)
HBM = pl.BlockSpec(memory_space=pltpu.HBM)


def moved(value, axis, count, steps):
    return lax.ppermute(value, axis, [(i, (i + steps) % count) for i in range(count)])


def shards(entities, hot_entities, relations, src_ids, rel_ids, dst_ids, neg_ids, counts, hot_slot):
    blocks = lax.axis_size(BLK)
    own = entities.T
    hot = hot_entities.T
    rel = relations.T
    sid = src_ids.reshape(1, -1)
    rid = rel_ids.reshape(1, -1)
    did = dst_ids.reshape(1, -1)
    nid = neg_ids.reshape(1, -1)
    count = counts.reshape(-1)
    slot = hot_slot.reshape(1, -1)
    core = lax.axis_index("core").astype(jnp.int32).reshape(1)
    after = moved(own, BLK, blocks, -1)
    before = moved(own, BLK, blocks, 1)
    edges = sid.shape[1]
    relg = pl.pallas_call(
        lookup_kernel,
        out_shape=struct((D, edges), BF16),
        in_specs=[VMEM, VMEM],
        out_specs=VMEM,
        compiler_params=PARAMS,
        cost_estimate=pl.CostEstimate(flops=3 * 10**9, bytes_accessed=10**7, transcendentals=0),
        name="lookup",
    )(rel, rid)
    half = struct((D, EDGES), BF16)
    block = struct((D, ENT), BF16)
    weight = struct((EDGES, HOT), BF16)
    src, low, low_t, gr1, own_grad, wh1 = pl.pallas_call(
        front_kernel,
        out_shape=(
            struct((D, edges), BF16), struct((D, edges), BF16), struct((edges, D), BF16),
            half, struct((D, ENT), F32), weight,
        ),
        in_specs=[VMEM] * 6 + [SMEM],
        out_specs=[VMEM] * 6,
        compiler_params=PARAMS,
        cost_estimate=COST,
        name="front",
    )(relg, own, hot, sid, did, nid, count)

    def back(k, far):
        return pl.pallas_call(
            functools.partial(back_kernel, k),
            out_shape=(half, half, weight, block),
            in_specs=[VMEM] * 8 + [SMEM],
            out_specs=[VMEM] * 4,
            compiler_params=PARAMS,
            cost_estimate=COST,
            name="back",
        )(far, hot, src, relg, low, low_t, did, nid, count)

    gs0, gr0, wh0, next_grad = back(0, after)
    from_prev = moved(next_grad, BLK, blocks, 1)
    gs2, gr2, wh2, prev_grad = back(2, before)
    from_next = moved(prev_grad, BLK, blocks, -1)
    msg, grads, hot_mine = pl.pallas_call(
        pack_kernel,
        out_shape=(
            struct((MSG_ROWS, LANES), BF16), struct((D, edges), BF16),
            struct((HOT_BLOCKS * 512, LANES), BF16),
        ),
        in_specs=[VMEM] * 9 + [SMEM],
        out_specs=[VMEM] * 3,
        compiler_params=PARAMS,
        cost_estimate=COST,
        name="pack",
    )(gr0, gr1, gr2, wh0, wh1, wh2, low, rid, slot, core)
    own_grad = pl.pallas_call(
        tail_kernel,
        out_shape=struct((D, ENT), F32),
        in_specs=[VMEM] * 4,
        out_specs=VMEM,
        compiler_params=PARAMS,
        cost_estimate=COST,
        name="tail",
    )(own_grad, gs0, gs2, sid)
    swap = [(0, 1), (1, 0)]
    got = lax.ppermute(msg, "core", swap)
    got, own_grad = lax.optimization_barrier((got, own_grad))
    slabs = pl.pallas_call(
        spread_kernel,
        out_shape=struct((GROUP, SLAB, LANES), BF16),
        in_specs=[VMEM] * 4 + [SMEM],
        out_specs=HBM,
        scratch_shapes=[
            pltpu.VMEM((D, 2 * edges), BF16),
            pltpu.VMEM((1, 2 * edges), jnp.int32),
            pltpu.VMEM((GROUP, SLAB, LANES), BF16),
            pltpu.SemaphoreType.DMA((NREL // 2 // SPREAD,)),
        ],
        compiler_params=PARAMS,
        cost_estimate=COST,
        name="spread",
    )(grads, rid, got, hot_mine, core)
    slabs, from_prev, from_next = lax.optimization_barrier((slabs, from_prev, from_next))
    slabs = lax.all_to_all(slabs, NEAR, 0, 0, tiled=True)
    part = (own_grad + from_prev.astype(F32) + from_next.astype(F32)).astype(BF16)
    slabs, part = lax.optimization_barrier((slabs, part))
    twin = lax.ppermute(part, "rep", swap)
    pieces = pl.pallas_call(
        near_sum_kernel,
        out_shape=struct((QUAD, PIECE, LANES), BF16),
        in_specs=[VMEM],
        out_specs=VMEM,
        compiler_params=PARAMS,
        name="near_sum",
    )(slabs)
    pieces = lax.all_to_all(pieces, "zh", 0, 0, tiled=True)
    pieces, twin = lax.optimization_barrier((pieces, twin))
    column, hot_grad = pl.pallas_call(
        quad_sum_kernel,
        out_shape=(struct((GROUP, HALF_D, LANES), BF16), struct((4, D), F32)),
        in_specs=[VMEM],
        out_specs=(VMEM, VMEM),
        compiler_params=PARAMS,
        name="quad_sum",
    )(pieces)
    mine = lax.all_to_all(column, NEAR, 0, 0, tiled=True)
    other = lax.ppermute(mine, "core", swap)
    relation_grad = merged(core, other, merged(core, mine, None))
    entity_grad = part.astype(F32) + twin.astype(F32)
    return entity_grad.T, relation_grad.T, hot_grad


def solution(mesh):
    inner = Mesh(mesh.devices.reshape(4, 2, 4, 2, 2, 2), BLK + ("rep",))
    return jax.shard_map(
        shards,
        mesh=inner,
        in_specs=(
            P(BLK, None),
            P(),
            P(),
            P(BLK, "rep", None, None),
            P(BLK, "rep", None, None),
            P(BLK, "rep", None, None),
            P(BLK, "rep", None, None),
            P(BLK, "rep", None),
            P(),
        ),
        out_specs=(P(BLK, None), P(), P(BLK + ("rep",), None)),
        check_vma=False,
    )
```

```python
import functools
import jax
import jax.numpy as jnp
import numpy as np
from jax import lax
from jax.experimental import pallas as pl
from jax.experimental.pallas import tpu as pltpu
from jax.sharding import Mesh, PartitionSpec as P

F32 = jnp.float32
BF16 = jnp.bfloat16
D = 400
HALF_D = 200
NREL = 4096
EDGES = 256
NEG = 512
ENT = 512
HOT = 1024
GROUP = 32
QUAD = 4
LANES = 128
REL_ROWS = D + 16
HOT_BASE = 6 * REL_ROWS
HOT_BLOCKS = 4
MSG_ROWS = HOT_BASE + HOT_BLOCKS * 512
TAIL = HALF_D
HOT_AT = HALF_D + 8
SLAB = HOT_AT + 3 * 16
WIDE = 256
SPREAD = 512
BLK = ("y", "xh", "zh", "zl", "core")
NEAR = ("y", "xh", "zl", "rep")


def onehot(rows, ids):
    grid = lax.broadcasted_iota(jnp.int32, (rows, ids.shape[1]), 0)
    return jnp.where(grid == ids, 1.0, 0.0).astype(BF16)


def dot(a, b):
    return lax.dot_general(a, b, (((1,), (0,)), ((), ())), preferred_element_type=F32)


def dot_nt(a, b):
    return lax.dot_general(a, b, (((1,), (1,)), ((), ())), preferred_element_type=F32)


def to_column(row):
    return jnp.transpose(jnp.broadcast_to(row, (8, row.shape[1])))[:, :1]


def to_row(column):
    return jnp.transpose(jnp.broadcast_to(column, (column.shape[0], LANES)))[:1]


def halves(value):
    return value[:HALF_D], value[HALF_D:]


def complex_product(left, right):
    lr, li = halves(left)
    rr, ri = halves(right)
    return jnp.concatenate([lr * rr - li * ri, lr * ri + li * rr], axis=0)


def conj_product(left, right):
    lr, li = halves(left)
    rr, ri = halves(right)
    return jnp.concatenate([lr * rr + li * ri, li * rr - lr * ri], axis=0)


def bucket_grads(src, rel, low, low_t, far, hot, dst, neg, count):
    src = src.astype(F32)
    rel = rel.astype(F32)
    product = complex_product(src, rel)
    dst_hot = onehot(ENT, dst)
    target = dot(far, dst_hot)
    positive = to_column(jnp.sum(product * target, axis=0, keepdims=True))
    table = dot_nt(
        onehot(16, jnp.right_shift(neg, 7)), onehot(LANES, jnp.bitwise_and(neg, LANES - 1))
    )
    times = jnp.concatenate(
        [table[i : i + 1] for i in range((ENT + HOT) // LANES)], axis=1
    )
    bias = jnp.where(times > 0.0, jnp.log(jnp.maximum(times, 1.0)), -1e30)
    score_far = dot(low_t, far) + bias[:, :ENT]
    score_hot = dot(low_t, hot) + bias[:, ENT:]
    peak = jnp.maximum(
        jnp.max(score_far, axis=1, keepdims=True), jnp.max(score_hot, axis=1, keepdims=True)
    )
    peak = jnp.maximum(peak, positive)
    exp_far = jnp.exp(score_far - peak)
    exp_hot = jnp.exp(score_hot - peak)
    exp_positive = jnp.exp(positive - peak)
    total = (
        exp_positive
        + jnp.sum(exp_far, axis=1, keepdims=True)
        + jnp.sum(exp_hot, axis=1, keepdims=True)
    )
    live = jnp.where(lax.broadcasted_iota(jnp.int32, (EDGES, 1), 0) < count, 1.0, 0.0)
    g_positive = to_row(live * (exp_positive / total - 1.0))
    scale = live / total
    w_far = (exp_far * scale).astype(BF16)
    w_hot = (exp_hot * scale).astype(BF16)
    g_product = g_positive * target + dot_nt(far, w_far) + dot_nt(hot, w_hot)
    g_source = conj_product(g_product, rel).astype(BF16)
    g_relation = conj_product(g_product, src).astype(BF16)
    g_target = (g_positive * product).astype(BF16)
    g_far = dot(low, w_far) + dot_nt(g_target, dst_hot)
    return g_source, g_relation, g_far, w_hot


def lookup_kernel(rel_ref, rid_ref, out_ref):
    for start in range(0, rid_ref.shape[1], WIDE):
        part = slice(start, start + WIDE)
        out_ref[:, part] = dot(rel_ref[...], onehot(NREL, rid_ref[:, part])).astype(BF16)


def front_kernel(
    rel_ref, own_ref, hot_ref, src_ref, dst_ref, neg_ref, count_ref,
    src_out, low_out, low_t_out, gr_out, own_out, wh_out,
):
    rel = rel_ref[...]
    places = onehot(ENT, src_ref[...])
    src = dot(own_ref[...], places)
    low = complex_product(src, rel.astype(F32)).astype(BF16)
    low_t = jnp.transpose(low.astype(F32)).astype(BF16)
    src = src.astype(BF16)
    src_out[...] = src
    low_out[...] = low
    low_t_out[...] = low_t
    hot = hot_ref[...]
    mid = slice(EDGES, 2 * EDGES)
    g_source, g_relation, g_far, w_hot = bucket_grads(
        src[:, mid], rel[:, mid], low[:, mid], low_t[mid], own_ref[...], hot,
        dst_ref[:, mid], neg_ref[:, NEG : 2 * NEG], count_ref[1],
    )
    gr_out[...] = g_relation
    own_out[...] = g_far + dot_nt(g_source, places[:, mid])
    wh_out[...] = w_hot


def back_kernel(
    k, far_ref, hot_ref, src_ref, rel_ref, low_ref, low_t_ref, dst_ref, neg_ref, count_ref,
    gs_out, gr_out, wh_out, far_out,
):
    part = slice(k * EDGES, (k + 1) * EDGES)
    g_source, g_relation, g_far, w_hot = bucket_grads(
        src_ref[:, part], rel_ref[:, part], low_ref[:, part], low_t_ref[part], far_ref[...],
        hot_ref[...], dst_ref[:, part], neg_ref[:, k * NEG : (k + 1) * NEG], count_ref[k],
    )
    gs_out[...] = g_source
    gr_out[...] = g_relation
    wh_out[...] = w_hot
    far_out[...] = g_far.astype(BF16)


def hot_rows(g_hot, slot, core, out, first):
    owner = jnp.right_shift(slot, 2)
    spot = (
        jnp.bitwise_and(jnp.right_shift(owner, 1), 1) * 512
        + jnp.right_shift(owner, 5) * 64
        + jnp.bitwise_and(jnp.right_shift(owner, 2), 1) * 32
        + jnp.bitwise_and(owner, 1) * 16
        + jnp.bitwise_and(jnp.right_shift(owner, 3), 3) * 4
        + jnp.bitwise_and(slot, 3)
    )
    rows = dot_nt(onehot(512, spot - core * 512), g_hot).astype(BF16)
    for b in range(3):
        start = first + b * 512
        out[start : start + 512, :] = rows[:, b * LANES : (b + 1) * LANES]
    out[first + 3 * 512 : first + 4 * 512, :] = jnp.concatenate(
        [rows[:, 3 * LANES :], jnp.zeros((512, HOT_BLOCKS * LANES - D), BF16)], axis=1
    )


def pack_kernel(
    gr0_ref, gr1_ref, gr2_ref, wh0_ref, wh1_ref, wh2_ref, low_ref, rid_ref, slot_ref, core_ref,
    msg_out, all_out, g_hot_out,
):
    relations = [gr0_ref[...], gr1_ref[...], gr2_ref[...]]
    weights = [wh0_ref[...], wh1_ref[...], wh2_ref[...]]
    rel_ids = rid_ref[...]
    place = lax.broadcasted_iota(jnp.int32, (16, LANES), 0)
    for b in range(6):
        ids = rel_ids[:, b * LANES : (b + 1) * LANES]
        high = jnp.right_shift(ids, 6).astype(F32)
        low = jnp.bitwise_and(ids, 63).astype(F32)
        tail = jnp.where(place == 0, high, jnp.where(place == 1, low, 0.0)).astype(BF16)
        piece = relations[b // 2][:, (b % 2) * LANES : (b % 2 + 1) * LANES]
        msg_out[b * REL_ROWS : b * REL_ROWS + D, :] = piece
        all_out[:, b * LANES : (b + 1) * LANES] = piece
        msg_out[b * REL_ROWS + D : (b + 1) * REL_ROWS, :] = tail
    g_hot = dot(low_ref[...], jnp.concatenate(weights, axis=0)).astype(BF16)
    g_hot_out[...] = g_hot
    hot_rows(g_hot, slot_ref[...], 1 - core_ref[0], msg_out, HOT_BASE)


def tail_kernel(
    own_ref, gs0_ref, gs2_ref, sid_ref, g_hot_ref, slot_ref, core_ref, own_out, hot_out
):
    ids = sid_ref[...]
    total = own_ref[...]
    for k, gs_ref in ((0, gs0_ref), (2, gs2_ref)):
        total = total + dot_nt(gs_ref[...], onehot(ENT, ids[:, k * EDGES : (k + 1) * EDGES]))
    own_out[...] = total
    hot_rows(g_hot_ref[...], slot_ref[...], core_ref[0], hot_out, 0)


def spread_kernel(grad_ref, rid_ref, got_ref, hot_ref, core_ref, out_ref, grads, id_ref, slabs, sems):
    edges = grad_ref.shape[1]
    grads[:, :edges] = grad_ref[...]
    id_ref[:, :edges] = rid_ref[...]
    for b in range(6):
        col = edges + b * LANES
        grads[:, col : col + LANES] = got_ref[b * REL_ROWS : b * REL_ROWS + D, :]
        tail = got_ref[b * REL_ROWS + D : (b + 1) * REL_ROWS, :].astype(F32)
        ids = tail[0:1] * 64.0 + tail[1:2]
        id_ref[:, col : col + LANES] = ids.astype(jnp.int32)
    ids = id_ref[...] - core_ref[0] * (NREL // 2)
    copies = []
    for i in range(NREL // 2 // SPREAD):
        wide = dot_nt(grads[...], onehot(SPREAD, ids - i * SPREAD))
        count = SPREAD // LANES
        for n in range(count):
            for zl in range(2):
                j = 2 * count * i + 4 * (n // 2) + 2 * zl + n % 2
                hot = []
                for b in range(HOT_BLOCKS):
                    row = b * 512 + j * 16
                    hot.append(
                        hot_ref[row : row + 16, :].astype(F32)
                        + got_ref[HOT_BASE + row : HOT_BASE + row + 16, :].astype(F32)
                    )
                last = hot.pop()
                tail = jnp.concatenate(
                    [last[:8, :16], last[8:, :16], jnp.zeros((8, LANES - 32), F32)], axis=1
                )
                piece = wide[zl * HALF_D : (zl + 1) * HALF_D, n * LANES : (n + 1) * LANES]
                slabs[j] = jnp.concatenate([piece, tail] + hot, axis=0).astype(BF16)
        part = pl.ds(2 * count * i, 2 * count)
        copy = pltpu.make_async_copy(slabs.at[part], out_ref.at[part], sems.at[i])
        copy.start()
        copies.append(copy)
    for copy in copies:
        copy.wait()


def near_sum_kernel(in_ref, out_ref):
    total = in_ref[0].astype(F32)
    for j in range(1, GROUP):
        total = total + in_ref[j].astype(F32)
    out_ref[...] = total.astype(BF16)


def quad_sum_kernel(r0, r1, r2, r3, place_ref, rel_ref, hot_ref, held):
    place = place_ref[0]
    for n, ref in enumerate((r0, r1, r2, r3)):
        held[n] = ref[...]
    total = None
    for source in range(QUAD):
        piece = held[jnp.bitwise_and(place - source, QUAD - 1)].astype(F32)
        total = piece if total is None else total + piece
    rel = total[:HALF_D].astype(BF16)
    for j in range(GROUP):
        rel_ref[j] = rel
    for q in range(QUAD):

        @pl.when(place == q)
        def _():
            for b in range(3):
                row = HOT_AT + b * 16 + q * 4
                hot_ref[:, b * LANES : (b + 1) * LANES] = total[row : row + 4]
            row, col = TAIL + (q % 2) * 4, (q // 2) * 16
            hot_ref[:, 3 * LANES :] = total[row : row + 4, col : col + 16]


def merge_kernel(core_ref, in_ref, *refs):
    out_ref = refs[-1]
    for near in range(in_ref.shape[0] // 4):
        for zl in range(2):
            for rep in range(2):
                col = (2 * near + rep) * LANES
                out_ref[zl * HALF_D : (zl + 1) * HALF_D, col : col + LANES] = in_ref[
                    4 * near + 2 * zl + rep
                ].astype(F32)


def merged(core, value, before):
    steps = GROUP // 16
    first = before is None
    if first:
        place = lambda i, c: (0, c[0] * steps + i)
    else:
        place = lambda i, c: (0, (1 - c[0]) * steps + i)
    in_specs = [pl.BlockSpec((16, HALF_D, LANES), lambda i, c: (i, 0, 0))]
    if not first:
        in_specs.append(pl.BlockSpec(memory_space=pl.ANY))
    return pl.pallas_call(
        merge_kernel,
        out_shape=struct((D, NREL), F32),
        grid_spec=pltpu.PrefetchScalarGridSpec(
            num_scalar_prefetch=1,
            grid=(steps,),
            in_specs=in_specs,
            out_specs=pl.BlockSpec((D, 8 * LANES), place),
        ),
        input_output_aliases={} if first else {2: 0},
        compiler_params=PARAMS,
        cost_estimate=pl.CostEstimate(flops=0, bytes_accessed=10**7, transcendentals=0),
        name="merge",
    )(core, value, *([] if first else [before]))


def struct(shape, dtype):
    return jax.ShapeDtypeStruct(shape, dtype)


COST = pl.CostEstimate(flops=10**8, bytes_accessed=10**6, transcendentals=0)
PARAMS = pltpu.CompilerParams(vmem_limit_bytes=28 * 1024 * 1024)
VMEM = pl.BlockSpec(memory_space=pltpu.VMEM)
SMEM = pl.BlockSpec(memory_space=pltpu.SMEM)
HBM = pl.BlockSpec(memory_space=pltpu.HBM)


def moved(value, axis, count, steps):
    return lax.ppermute(value, axis, [(i, (i + steps) % count) for i in range(count)])


def shards(entities, hot_entities, relations, src_ids, rel_ids, dst_ids, neg_ids, counts, hot_slot):
    blocks = lax.axis_size(BLK)
    own = entities.T
    hot = hot_entities.T
    rel = relations.T
    sid = src_ids.reshape(1, -1)
    rid = rel_ids.reshape(1, -1)
    did = dst_ids.reshape(1, -1)
    nid = neg_ids.reshape(1, -1)
    count = counts.reshape(-1)
    slot = hot_slot.reshape(1, -1)
    core = lax.axis_index("core").astype(jnp.int32).reshape(1)
    after = moved(own, BLK, blocks, -1)
    before = moved(own, BLK, blocks, 1)
    edges = sid.shape[1]
    relg = pl.pallas_call(
        lookup_kernel,
        out_shape=struct((D, edges), BF16),
        in_specs=[VMEM, VMEM],
        out_specs=VMEM,
        compiler_params=PARAMS,
        cost_estimate=pl.CostEstimate(flops=3 * 10**9, bytes_accessed=10**7, transcendentals=0),
        name="lookup",
    )(rel, rid)
    half = struct((D, EDGES), BF16)
    block = struct((D, ENT), BF16)
    weight = struct((EDGES, HOT), BF16)
    src, low, low_t, gr1, own_grad, wh1 = pl.pallas_call(
        front_kernel,
        out_shape=(
            struct((D, edges), BF16), struct((D, edges), BF16), struct((edges, D), BF16),
            half, struct((D, ENT), F32), weight,
        ),
        in_specs=[VMEM] * 6 + [SMEM],
        out_specs=[VMEM] * 6,
        compiler_params=PARAMS,
        cost_estimate=COST,
        name="front",
    )(relg, own, hot, sid, did, nid, count)

    def back(k, far):
        return pl.pallas_call(
            functools.partial(back_kernel, k),
            out_shape=(half, half, weight, block),
            in_specs=[VMEM] * 8 + [SMEM],
            out_specs=[VMEM] * 4,
            compiler_params=PARAMS,
            cost_estimate=COST,
            name="back",
        )(far, hot, src, relg, low, low_t, did, nid, count)

    gs0, gr0, wh0, next_grad = back(0, after)
    from_prev = moved(next_grad, BLK, blocks, 1)
    gs2, gr2, wh2, prev_grad = back(2, before)
    from_next = moved(prev_grad, BLK, blocks, -1)
    msg, grads, g_hot = pl.pallas_call(
        pack_kernel,
        out_shape=(
            struct((MSG_ROWS, LANES), BF16), struct((D, edges), BF16),
            struct((D, HOT), BF16),
        ),
        in_specs=[VMEM] * 9 + [SMEM],
        out_specs=[VMEM] * 3,
        compiler_params=PARAMS,
        cost_estimate=COST,
        name="pack",
    )(gr0, gr1, gr2, wh0, wh1, wh2, low, rid, slot, core)
    own_grad, hot_mine = pl.pallas_call(
        tail_kernel,
        out_shape=(struct((D, ENT), F32), struct((HOT_BLOCKS * 512, LANES), BF16)),
        in_specs=[VMEM] * 6 + [SMEM],
        out_specs=[VMEM] * 2,
        compiler_params=PARAMS,
        cost_estimate=COST,
        name="tail",
    )(own_grad, gs0, gs2, sid, g_hot, slot, core)
    swap = [(0, 1), (1, 0)]
    got = lax.ppermute(msg, "core", swap)
    got, own_grad, hot_mine = lax.optimization_barrier((got, own_grad, hot_mine))
    slabs = pl.pallas_call(
        spread_kernel,
        out_shape=struct((GROUP, SLAB, LANES), BF16),
        in_specs=[VMEM] * 4 + [SMEM],
        out_specs=HBM,
        scratch_shapes=[
            pltpu.VMEM((D, 2 * edges), BF16),
            pltpu.VMEM((1, 2 * edges), jnp.int32),
            pltpu.VMEM((GROUP, SLAB, LANES), BF16),
            pltpu.SemaphoreType.DMA((NREL // 2 // SPREAD,)),
        ],
        compiler_params=PARAMS,
        cost_estimate=COST,
        name="spread",
    )(grads, rid, got, hot_mine, core)
    slabs, from_prev, from_next = lax.optimization_barrier((slabs, from_prev, from_next))
    slabs = lax.all_to_all(slabs, NEAR, 0, 0, tiled=True)
    part = (own_grad + from_prev.astype(F32) + from_next.astype(F32)).astype(BF16)
    slabs, part = lax.optimization_barrier((slabs, part))
    twin = lax.ppermute(part, "rep", swap)
    pieces = pl.pallas_call(
        near_sum_kernel,
        out_shape=struct((SLAB, LANES), BF16),
        in_specs=[VMEM],
        out_specs=VMEM,
        compiler_params=PARAMS,
        name="near_sum",
    )(slabs)
    pieces = [pieces] + [moved(pieces, "zh", QUAD, n) for n in range(1, QUAD)]
    place = lax.axis_index("zh").astype(jnp.int32).reshape(1)
    pieces, twin = lax.optimization_barrier((pieces, twin))
    column, hot_grad = pl.pallas_call(
        quad_sum_kernel,
        out_shape=(struct((GROUP, HALF_D, LANES), BF16), struct((4, D), F32)),
        in_specs=[VMEM] * QUAD + [SMEM],
        out_specs=(VMEM, VMEM),
        scratch_shapes=[pltpu.VMEM((QUAD, SLAB, LANES), BF16)],
        compiler_params=PARAMS,
        name="quad_sum",
    )(*pieces, place)
    mine = lax.all_to_all(column, NEAR, 0, 0, tiled=True)
    other = lax.ppermute(mine, "core", swap)
    relation_grad = merged(core, other, merged(core, mine, None))
    entity_grad = part.astype(F32) + twin.astype(F32)
    return entity_grad.T, relation_grad.T, hot_grad


def solution(mesh):
    inner = Mesh(mesh.devices.reshape(4, 2, 4, 2, 2, 2), BLK + ("rep",))
    return jax.shard_map(
        shards,
        mesh=inner,
        in_specs=(
            P(BLK, None),
            P(),
            P(),
            P(BLK, "rep", None, None),
            P(BLK, "rep", None, None),
            P(BLK, "rep", None, None),
            P(BLK, "rep", None, None),
            P(BLK, "rep", None),
            P(),
        ),
        out_specs=(P(BLK, None), P(), P(BLK + ("rep",), None)),
        check_vma=False,
    )
```

```python
import functools
import jax
import jax.numpy as jnp
import numpy as np
from jax import lax
from jax.experimental import pallas as pl
from jax.experimental.pallas import tpu as pltpu
from jax.sharding import Mesh, PartitionSpec as P

F32 = jnp.float32
BF16 = jnp.bfloat16
D = 400
HALF_D = 200
NREL = 4096
EDGES = 256
NEG = 512
ENT = 512
HOT = 1024
GROUP = 32
QUAD = 4
LANES = 128
REL_ROWS = D + 16
HOT_BASE = 6 * REL_ROWS
HOT_BLOCKS = 4
MSG_ROWS = HOT_BASE + HOT_BLOCKS * 512
TAIL = HALF_D
HOT_AT = HALF_D + 8
SLAB = HOT_AT + 3 * 16
WIDE = 256
SPREAD = 512
BLK = ("y", "xh", "zh", "zl", "core")
NEAR = ("y", "xh", "zl", "rep")


def onehot(rows, ids):
    grid = lax.broadcasted_iota(jnp.int32, (rows, ids.shape[1]), 0)
    return jnp.where(grid == ids, 1.0, 0.0).astype(BF16)


def dot(a, b):
    return lax.dot_general(a, b, (((1,), (0,)), ((), ())), preferred_element_type=F32)


def dot_nt(a, b):
    return lax.dot_general(a, b, (((1,), (1,)), ((), ())), preferred_element_type=F32)


def to_column(row):
    return jnp.transpose(jnp.broadcast_to(row, (8, row.shape[1])))[:, :1]


def to_row(column):
    return jnp.transpose(jnp.broadcast_to(column, (column.shape[0], LANES)))[:1]


def halves(value):
    return value[:HALF_D], value[HALF_D:]


def complex_product(left, right):
    lr, li = halves(left)
    rr, ri = halves(right)
    return jnp.concatenate([lr * rr - li * ri, lr * ri + li * rr], axis=0)


def conj_product(left, right):
    lr, li = halves(left)
    rr, ri = halves(right)
    return jnp.concatenate([lr * rr + li * ri, li * rr - lr * ri], axis=0)


def bucket_grads(src, rel, low, low_t, far, hot, dst, neg, count):
    src = src.astype(F32)
    rel = rel.astype(F32)
    product = complex_product(src, rel)
    dst_hot = onehot(ENT, dst)
    target = dot(far, dst_hot)
    positive = to_column(jnp.sum(product * target, axis=0, keepdims=True))
    table = dot_nt(
        onehot(16, jnp.right_shift(neg, 7)), onehot(LANES, jnp.bitwise_and(neg, LANES - 1))
    )
    times = jnp.concatenate(
        [table[i : i + 1] for i in range((ENT + HOT) // LANES)], axis=1
    )
    bias = jnp.where(times > 0.0, jnp.log(jnp.maximum(times, 1.0)), -1e30)
    score_far = dot(low_t, far) + bias[:, :ENT]
    score_hot = dot(low_t, hot) + bias[:, ENT:]
    peak = jnp.maximum(
        jnp.max(score_far, axis=1, keepdims=True), jnp.max(score_hot, axis=1, keepdims=True)
    )
    peak = jnp.maximum(peak, positive)
    exp_far = jnp.exp(score_far - peak)
    exp_hot = jnp.exp(score_hot - peak)
    exp_positive = jnp.exp(positive - peak)
    total = (
        exp_positive
        + jnp.sum(exp_far, axis=1, keepdims=True)
        + jnp.sum(exp_hot, axis=1, keepdims=True)
    )
    live = jnp.where(lax.broadcasted_iota(jnp.int32, (EDGES, 1), 0) < count, 1.0, 0.0)
    g_positive = to_row(live * (exp_positive / total - 1.0))
    scale = live / total
    w_far = (exp_far * scale).astype(BF16)
    w_hot = (exp_hot * scale).astype(BF16)
    g_product = g_positive * target + dot_nt(far, w_far) + dot_nt(hot, w_hot)
    g_source = conj_product(g_product, rel).astype(BF16)
    g_relation = conj_product(g_product, src).astype(BF16)
    g_target = (g_positive * product).astype(BF16)
    g_far = dot(low, w_far) + dot_nt(g_target, dst_hot)
    return g_source, g_relation, g_far, w_hot


def lookup_kernel(rel_ref, rid_ref, out_ref):
    for start in range(0, rid_ref.shape[1], WIDE):
        part = slice(start, start + WIDE)
        out_ref[:, part] = dot(rel_ref[...], onehot(NREL, rid_ref[:, part])).astype(BF16)


def front_kernel(
    rel_ref, own_ref, hot_ref, src_ref, dst_ref, neg_ref, count_ref,
    src_out, low_out, low_t_out, gr_out, own_out, wh_out,
):
    rel = rel_ref[...]
    places = onehot(ENT, src_ref[...])
    src = dot(own_ref[...], places)
    low = complex_product(src, rel.astype(F32)).astype(BF16)
    low_t = jnp.transpose(low.astype(F32)).astype(BF16)
    src = src.astype(BF16)
    src_out[...] = src
    low_out[...] = low
    low_t_out[...] = low_t
    hot = hot_ref[...]
    mid = slice(EDGES, 2 * EDGES)
    g_source, g_relation, g_far, w_hot = bucket_grads(
        src[:, mid], rel[:, mid], low[:, mid], low_t[mid], own_ref[...], hot,
        dst_ref[:, mid], neg_ref[:, NEG : 2 * NEG], count_ref[1],
    )
    gr_out[...] = g_relation
    own_out[...] = g_far + dot_nt(g_source, places[:, mid])
    wh_out[...] = w_hot


def back_kernel(
    k, far_ref, hot_ref, src_ref, rel_ref, low_ref, low_t_ref, dst_ref, neg_ref, count_ref,
    gs_out, gr_out, wh_out, far_out,
):
    part = slice(k * EDGES, (k + 1) * EDGES)
    g_source, g_relation, g_far, w_hot = bucket_grads(
        src_ref[:, part], rel_ref[:, part], low_ref[:, part], low_t_ref[part], far_ref[...],
        hot_ref[...], dst_ref[:, part], neg_ref[:, k * NEG : (k + 1) * NEG], count_ref[k],
    )
    gs_out[...] = g_source
    gr_out[...] = g_relation
    wh_out[...] = w_hot
    far_out[...] = g_far.astype(BF16)


def hot_rows(g_hot, slot, core, out, first):
    owner = jnp.right_shift(slot, 2)
    spot = (
        jnp.bitwise_and(jnp.right_shift(owner, 1), 1) * 512
        + jnp.right_shift(owner, 5) * 64
        + jnp.bitwise_and(jnp.right_shift(owner, 2), 1) * 32
        + jnp.bitwise_and(owner, 1) * 16
        + jnp.bitwise_and(jnp.right_shift(owner, 3), 3) * 4
        + jnp.bitwise_and(slot, 3)
    )
    rows = dot_nt(onehot(512, spot - core * 512), g_hot).astype(BF16)
    for b in range(3):
        start = first + b * 512
        out[start : start + 512, :] = rows[:, b * LANES : (b + 1) * LANES]
    out[first + 3 * 512 : first + 4 * 512, :] = jnp.concatenate(
        [rows[:, 3 * LANES :], jnp.zeros((512, HOT_BLOCKS * LANES - D), BF16)], axis=1
    )


def pack_kernel(
    gr0_ref, gr1_ref, gr2_ref, wh0_ref, wh1_ref, wh2_ref, low_ref, rid_ref, slot_ref, core_ref,
    msg_out, all_out, g_hot_out,
):
    relations = [gr0_ref[...], gr1_ref[...], gr2_ref[...]]
    weights = [wh0_ref[...], wh1_ref[...], wh2_ref[...]]
    rel_ids = rid_ref[...]
    place = lax.broadcasted_iota(jnp.int32, (16, LANES), 0)
    for b in range(6):
        ids = rel_ids[:, b * LANES : (b + 1) * LANES]
        high = jnp.right_shift(ids, 6).astype(F32)
        low = jnp.bitwise_and(ids, 63).astype(F32)
        tail = jnp.where(place == 0, high, jnp.where(place == 1, low, 0.0)).astype(BF16)
        piece = relations[b // 2][:, (b % 2) * LANES : (b % 2 + 1) * LANES]
        msg_out[b * REL_ROWS : b * REL_ROWS + D, :] = piece
        all_out[:, b * LANES : (b + 1) * LANES] = piece
        msg_out[b * REL_ROWS + D : (b + 1) * REL_ROWS, :] = tail
    g_hot = dot(low_ref[...], jnp.concatenate(weights, axis=0)).astype(BF16)
    g_hot_out[...] = g_hot
    hot_rows(g_hot, slot_ref[...], 1 - core_ref[0], msg_out, HOT_BASE)


def tail_kernel(
    own_ref, gs0_ref, gs2_ref, sid_ref, g_hot_ref, slot_ref, core_ref, own_out, hot_out
):
    ids = sid_ref[...]
    total = own_ref[...]
    for k, gs_ref in ((0, gs0_ref), (2, gs2_ref)):
        total = total + dot_nt(gs_ref[...], onehot(ENT, ids[:, k * EDGES : (k + 1) * EDGES]))
    own_out[...] = total
    hot_rows(g_hot_ref[...], slot_ref[...], core_ref[0], hot_out, 0)


def spread_kernel(grad_ref, rid_ref, got_ref, hot_ref, core_ref, out_ref, grads, id_ref, slabs, sems):
    edges = grad_ref.shape[1]
    grads[:, :edges] = grad_ref[...]
    id_ref[:, :edges] = rid_ref[...]
    for b in range(6):
        col = edges + b * LANES
        grads[:, col : col + LANES] = got_ref[b * REL_ROWS : b * REL_ROWS + D, :]
        tail = got_ref[b * REL_ROWS + D : (b + 1) * REL_ROWS, :].astype(F32)
        ids = tail[0:1] * 64.0 + tail[1:2]
        id_ref[:, col : col + LANES] = ids.astype(jnp.int32)
    ids = id_ref[...] - core_ref[0] * (NREL // 2)
    copies = []
    for i in range(NREL // 2 // SPREAD):
        wide = dot_nt(grads[...], onehot(SPREAD, ids - i * SPREAD))
        count = SPREAD // LANES
        for n in range(count):
            for zl in range(2):
                j = 2 * count * i + 4 * (n // 2) + 2 * zl + n % 2
                hot = []
                for b in range(HOT_BLOCKS):
                    row = b * 512 + j * 16
                    hot.append(
                        hot_ref[row : row + 16, :].astype(F32)
                        + got_ref[HOT_BASE + row : HOT_BASE + row + 16, :].astype(F32)
                    )
                last = hot.pop()
                tail = jnp.concatenate(
                    [last[:8, :16], last[8:, :16], jnp.zeros((8, LANES - 32), F32)], axis=1
                )
                piece = wide[zl * HALF_D : (zl + 1) * HALF_D, n * LANES : (n + 1) * LANES]
                slabs[j] = jnp.concatenate([piece, tail] + hot, axis=0).astype(BF16)
        part = pl.ds(2 * count * i, 2 * count)
        copy = pltpu.make_async_copy(slabs.at[part], out_ref.at[part], sems.at[i])
        copy.start()
        copies.append(copy)
    for copy in copies:
        copy.wait()


def near_sum_kernel(in_ref, out_ref):
    total = in_ref[0].astype(F32)
    for j in range(1, GROUP):
        total = total + in_ref[j].astype(F32)
    out_ref[...] = total.astype(BF16)


def pair_sum_kernel(mine_ref, got_ref, out_ref):
    out_ref[...] = (mine_ref[...].astype(F32) + got_ref[...].astype(F32)).astype(BF16)


def quad_sum_kernel(mine_ref, got_ref, place_ref, rel_ref, hot_ref):
    place = place_ref[0]
    total = mine_ref[...].astype(F32) + got_ref[...].astype(F32)
    rel = total[:HALF_D].astype(BF16)
    for j in range(GROUP):
        rel_ref[j] = rel
    for q in range(QUAD):

        @pl.when(place == q)
        def _():
            for b in range(3):
                row = HOT_AT + b * 16 + q * 4
                hot_ref[:, b * LANES : (b + 1) * LANES] = total[row : row + 4]
            row, col = TAIL + (q % 2) * 4, (q // 2) * 16
            hot_ref[:, 3 * LANES :] = total[row : row + 4, col : col + 16]


def merge_kernel(core_ref, in_ref, *refs):
    out_ref = refs[-1]
    for near in range(in_ref.shape[0] // 4):
        for zl in range(2):
            for rep in range(2):
                col = (2 * near + rep) * LANES
                out_ref[zl * HALF_D : (zl + 1) * HALF_D, col : col + LANES] = in_ref[
                    4 * near + 2 * zl + rep
                ].astype(F32)


def merged(core, value, before):
    steps = GROUP // 16
    first = before is None
    if first:
        place = lambda i, c: (0, c[0] * steps + i)
    else:
        place = lambda i, c: (0, (1 - c[0]) * steps + i)
    in_specs = [pl.BlockSpec((16, HALF_D, LANES), lambda i, c: (i, 0, 0))]
    if not first:
        in_specs.append(pl.BlockSpec(memory_space=pl.ANY))
    return pl.pallas_call(
        merge_kernel,
        out_shape=struct((D, NREL), F32),
        grid_spec=pltpu.PrefetchScalarGridSpec(
            num_scalar_prefetch=1,
            grid=(steps,),
            in_specs=in_specs,
            out_specs=pl.BlockSpec((D, 8 * LANES), place),
        ),
        input_output_aliases={} if first else {2: 0},
        compiler_params=PARAMS,
        cost_estimate=pl.CostEstimate(flops=0, bytes_accessed=10**7, transcendentals=0),
        name="merge",
    )(core, value, *([] if first else [before]))


def struct(shape, dtype):
    return jax.ShapeDtypeStruct(shape, dtype)


COST = pl.CostEstimate(flops=10**8, bytes_accessed=10**6, transcendentals=0)
PARAMS = pltpu.CompilerParams(vmem_limit_bytes=28 * 1024 * 1024)
VMEM = pl.BlockSpec(memory_space=pltpu.VMEM)
SMEM = pl.BlockSpec(memory_space=pltpu.SMEM)
HBM = pl.BlockSpec(memory_space=pltpu.HBM)


def moved(value, axis, count, steps):
    return lax.ppermute(value, axis, [(i, (i + steps) % count) for i in range(count)])


def shards(entities, hot_entities, relations, src_ids, rel_ids, dst_ids, neg_ids, counts, hot_slot):
    blocks = lax.axis_size(BLK)
    own = entities.T
    hot = hot_entities.T
    rel = relations.T
    sid = src_ids.reshape(1, -1)
    rid = rel_ids.reshape(1, -1)
    did = dst_ids.reshape(1, -1)
    nid = neg_ids.reshape(1, -1)
    count = counts.reshape(-1)
    slot = hot_slot.reshape(1, -1)
    core = lax.axis_index("core").astype(jnp.int32).reshape(1)
    after = moved(own, BLK, blocks, -1)
    before = moved(own, BLK, blocks, 1)
    edges = sid.shape[1]
    relg = pl.pallas_call(
        lookup_kernel,
        out_shape=struct((D, edges), BF16),
        in_specs=[VMEM, VMEM],
        out_specs=VMEM,
        compiler_params=PARAMS,
        cost_estimate=pl.CostEstimate(flops=3 * 10**9, bytes_accessed=10**7, transcendentals=0),
        name="lookup",
    )(rel, rid)
    half = struct((D, EDGES), BF16)
    block = struct((D, ENT), BF16)
    weight = struct((EDGES, HOT), BF16)
    src, low, low_t, gr1, own_grad, wh1 = pl.pallas_call(
        front_kernel,
        out_shape=(
            struct((D, edges), BF16), struct((D, edges), BF16), struct((edges, D), BF16),
            half, struct((D, ENT), F32), weight,
        ),
        in_specs=[VMEM] * 6 + [SMEM],
        out_specs=[VMEM] * 6,
        compiler_params=PARAMS,
        cost_estimate=COST,
        name="front",
    )(relg, own, hot, sid, did, nid, count)

    def back(k, far):
        return pl.pallas_call(
            functools.partial(back_kernel, k),
            out_shape=(half, half, weight, block),
            in_specs=[VMEM] * 8 + [SMEM],
            out_specs=[VMEM] * 4,
            compiler_params=PARAMS,
            cost_estimate=COST,
            name="back",
        )(far, hot, src, relg, low, low_t, did, nid, count)

    gs0, gr0, wh0, next_grad = back(0, after)
    from_prev = moved(next_grad, BLK, blocks, 1)
    gs2, gr2, wh2, prev_grad = back(2, before)
    from_next = moved(prev_grad, BLK, blocks, -1)
    msg, grads, g_hot = pl.pallas_call(
        pack_kernel,
        out_shape=(
            struct((MSG_ROWS, LANES), BF16), struct((D, edges), BF16),
            struct((D, HOT), BF16),
        ),
        in_specs=[VMEM] * 9 + [SMEM],
        out_specs=[VMEM] * 3,
        compiler_params=PARAMS,
        cost_estimate=COST,
        name="pack",
    )(gr0, gr1, gr2, wh0, wh1, wh2, low, rid, slot, core)
    own_grad, hot_mine = pl.pallas_call(
        tail_kernel,
        out_shape=(struct((D, ENT), F32), struct((HOT_BLOCKS * 512, LANES), BF16)),
        in_specs=[VMEM] * 6 + [SMEM],
        out_specs=[VMEM] * 2,
        compiler_params=PARAMS,
        cost_estimate=COST,
        name="tail",
    )(own_grad, gs0, gs2, sid, g_hot, slot, core)
    swap = [(0, 1), (1, 0)]
    got = lax.ppermute(msg, "core", swap)
    got, own_grad, hot_mine = lax.optimization_barrier((got, own_grad, hot_mine))
    slabs = pl.pallas_call(
        spread_kernel,
        out_shape=struct((GROUP, SLAB, LANES), BF16),
        in_specs=[VMEM] * 4 + [SMEM],
        out_specs=HBM,
        scratch_shapes=[
            pltpu.VMEM((D, 2 * edges), BF16),
            pltpu.VMEM((1, 2 * edges), jnp.int32),
            pltpu.VMEM((GROUP, SLAB, LANES), BF16),
            pltpu.SemaphoreType.DMA((NREL // 2 // SPREAD,)),
        ],
        compiler_params=PARAMS,
        cost_estimate=COST,
        name="spread",
    )(grads, rid, got, hot_mine, core)
    slabs, from_prev, from_next = lax.optimization_barrier((slabs, from_prev, from_next))
    slabs = lax.all_to_all(slabs, NEAR, 0, 0, tiled=True)
    part = (own_grad + from_prev.astype(F32) + from_next.astype(F32)).astype(BF16)
    slabs, part = lax.optimization_barrier((slabs, part))
    twin = lax.ppermute(part, "rep", swap)
    pieces = pl.pallas_call(
        near_sum_kernel,
        out_shape=struct((SLAB, LANES), BF16),
        in_specs=[VMEM],
        out_specs=VMEM,
        compiler_params=PARAMS,
        name="near_sum",
    )(slabs)
    beside = lax.ppermute(pieces, "zh", [(i, i ^ 1) for i in range(QUAD)])
    pieces = pl.pallas_call(
        pair_sum_kernel,
        out_shape=struct((SLAB, LANES), BF16),
        in_specs=[VMEM] * 2,
        out_specs=VMEM,
        compiler_params=PARAMS,
        name="pair_sum",
    )(pieces, beside)
    across = lax.ppermute(pieces, "zh", [(i, i ^ 3) for i in range(QUAD)])
    place = lax.axis_index("zh").astype(jnp.int32).reshape(1)
    across, twin = lax.optimization_barrier((across, twin))
    column, hot_grad = pl.pallas_call(
        quad_sum_kernel,
        out_shape=(struct((GROUP, HALF_D, LANES), BF16), struct((4, D), F32)),
        in_specs=[VMEM] * 2 + [SMEM],
        out_specs=(VMEM, VMEM),
        compiler_params=PARAMS,
        name="quad_sum",
    )(pieces, across, place)
    mine = lax.all_to_all(column, NEAR, 0, 0, tiled=True)
    other = lax.ppermute(mine, "core", swap)
    relation_grad = merged(core, other, merged(core, mine, None))
    entity_grad = part.astype(F32) + twin.astype(F32)
    return entity_grad.T, relation_grad.T, hot_grad


def solution(mesh):
    inner = Mesh(mesh.devices.reshape(4, 2, 4, 2, 2, 2), BLK + ("rep",))
    return jax.shard_map(
        shards,
        mesh=inner,
        in_specs=(
            P(BLK, None),
            P(),
            P(),
            P(BLK, "rep", None, None),
            P(BLK, "rep", None, None),
            P(BLK, "rep", None, None),
            P(BLK, "rep", None, None),
            P(BLK, "rep", None),
            P(),
        ),
        out_specs=(P(BLK, None), P(), P(BLK + ("rep",), None)),
        check_vma=False,
    )
```

```python
import functools
import jax
import jax.numpy as jnp
import numpy as np
from jax import lax
from jax.experimental import pallas as pl
from jax.experimental.pallas import tpu as pltpu
from jax.sharding import Mesh, PartitionSpec as P

F32 = jnp.float32
BF16 = jnp.bfloat16
D = 400
HALF_D = 200
NREL = 4096
EDGES = 256
NEG = 512
ENT = 512
HOT = 1024
GROUP = 32
QUAD = 4
LANES = 128
REL_ROWS = D + 16
HOT_BASE = 6 * REL_ROWS
HOT_BLOCKS = 4
MSG_ROWS = HOT_BASE + HOT_BLOCKS * 512
TAIL = HALF_D
HOT_AT = HALF_D + 8
SLAB = HOT_AT + 3 * 16
WIDE = 256
SPREAD = 512
BLK = ("y", "xh", "zh", "zl", "core")
NEAR = ("y", "xh", "zl", "rep")


def onehot(rows, ids):
    grid = lax.broadcasted_iota(jnp.int32, (rows, ids.shape[1]), 0)
    return jnp.where(grid == ids, 1.0, 0.0).astype(BF16)


def dot(a, b):
    return lax.dot_general(a, b, (((1,), (0,)), ((), ())), preferred_element_type=F32)


def dot_nt(a, b):
    return lax.dot_general(a, b, (((1,), (1,)), ((), ())), preferred_element_type=F32)


def to_column(row):
    return jnp.transpose(jnp.broadcast_to(row, (8, row.shape[1])))[:, :1]


def to_row(column):
    return jnp.transpose(jnp.broadcast_to(column, (column.shape[0], LANES)))[:1]


def halves(value):
    return value[:HALF_D], value[HALF_D:]


def complex_product(left, right):
    lr, li = halves(left)
    rr, ri = halves(right)
    return jnp.concatenate([lr * rr - li * ri, lr * ri + li * rr], axis=0)


def conj_product(left, right):
    lr, li = halves(left)
    rr, ri = halves(right)
    return jnp.concatenate([lr * rr + li * ri, li * rr - lr * ri], axis=0)


def bucket_grads(src, rel, low, low_t, far, hot, dst, neg, count):
    src = src.astype(F32)
    rel = rel.astype(F32)
    product = complex_product(src, rel)
    dst_hot = onehot(ENT, dst)
    target = dot(far, dst_hot)
    positive = to_column(jnp.sum(product * target, axis=0, keepdims=True))
    table = dot_nt(
        onehot(16, jnp.right_shift(neg, 7)), onehot(LANES, jnp.bitwise_and(neg, LANES - 1))
    )
    times = jnp.concatenate(
        [table[i : i + 1] for i in range((ENT + HOT) // LANES)], axis=1
    )
    bias = jnp.where(times > 0.0, jnp.log(jnp.maximum(times, 1.0)), -1e30)
    score_far = dot(low_t, far) + bias[:, :ENT]
    score_hot = dot(low_t, hot) + bias[:, ENT:]
    peak = jnp.maximum(
        jnp.max(score_far, axis=1, keepdims=True), jnp.max(score_hot, axis=1, keepdims=True)
    )
    peak = jnp.maximum(peak, positive)
    exp_far = jnp.exp(score_far - peak)
    exp_hot = jnp.exp(score_hot - peak)
    exp_positive = jnp.exp(positive - peak)
    total = (
        exp_positive
        + jnp.sum(exp_far, axis=1, keepdims=True)
        + jnp.sum(exp_hot, axis=1, keepdims=True)
    )
    live = jnp.where(lax.broadcasted_iota(jnp.int32, (EDGES, 1), 0) < count, 1.0, 0.0)
    g_positive = to_row(live * (exp_positive / total - 1.0))
    scale = live / total
    w_far = (exp_far * scale).astype(BF16)
    w_hot = (exp_hot * scale).astype(BF16)
    g_product = g_positive * target + dot_nt(far, w_far) + dot_nt(hot, w_hot)
    g_source = conj_product(g_product, rel).astype(BF16)
    g_relation = conj_product(g_product, src).astype(BF16)
    g_target = (g_positive * product).astype(BF16)
    g_far = dot(low, w_far) + dot_nt(g_target, dst_hot)
    return g_source, g_relation, g_far, w_hot


def lookup_kernel(rel_ref, rid_ref, out_ref):
    for start in range(0, rid_ref.shape[1], WIDE):
        part = slice(start, start + WIDE)
        out_ref[:, part] = dot(rel_ref[...], onehot(NREL, rid_ref[:, part])).astype(BF16)


def front_kernel(
    rel_ref, own_ref, hot_ref, src_ref, dst_ref, neg_ref, count_ref,
    src_out, low_out, low_t_out, gr_out, own_out, wh_out,
):
    rel = rel_ref[...]
    places = onehot(ENT, src_ref[...])
    src = dot(own_ref[...], places)
    low = complex_product(src, rel.astype(F32)).astype(BF16)
    low_t = jnp.transpose(low.astype(F32)).astype(BF16)
    src = src.astype(BF16)
    src_out[...] = src
    low_out[...] = low
    low_t_out[...] = low_t
    hot = hot_ref[...]
    mid = slice(EDGES, 2 * EDGES)
    g_source, g_relation, g_far, w_hot = bucket_grads(
        src[:, mid], rel[:, mid], low[:, mid], low_t[mid], own_ref[...], hot,
        dst_ref[:, mid], neg_ref[:, NEG : 2 * NEG], count_ref[1],
    )
    gr_out[...] = g_relation
    own_out[...] = g_far + dot_nt(g_source, places[:, mid])
    wh_out[...] = w_hot


def back_kernel(
    k, far_ref, hot_ref, src_ref, rel_ref, low_ref, low_t_ref, dst_ref, neg_ref, count_ref,
    gs_out, gr_out, wh_out, far_out,
):
    part = slice(k * EDGES, (k + 1) * EDGES)
    g_source, g_relation, g_far, w_hot = bucket_grads(
        src_ref[:, part], rel_ref[:, part], low_ref[:, part], low_t_ref[part], far_ref[...],
        hot_ref[...], dst_ref[:, part], neg_ref[:, k * NEG : (k + 1) * NEG], count_ref[k],
    )
    gs_out[...] = g_source
    gr_out[...] = g_relation
    wh_out[...] = w_hot
    far_out[...] = g_far.astype(BF16)


def hot_rows(g_hot, slot, core, out, first):
    owner = jnp.right_shift(slot, 2)
    spot = (
        jnp.bitwise_and(jnp.right_shift(owner, 1), 1) * 512
        + jnp.right_shift(owner, 5) * 64
        + jnp.bitwise_and(jnp.right_shift(owner, 2), 1) * 32
        + jnp.bitwise_and(owner, 1) * 16
        + jnp.bitwise_and(jnp.right_shift(owner, 3), 3) * 4
        + jnp.bitwise_and(slot, 3)
    )
    rows = dot_nt(onehot(512, spot - core * 512), g_hot).astype(BF16)
    for b in range(3):
        start = first + b * 512
        out[start : start + 512, :] = rows[:, b * LANES : (b + 1) * LANES]
    out[first + 3 * 512 : first + 4 * 512, :] = jnp.concatenate(
        [rows[:, 3 * LANES :], jnp.zeros((512, HOT_BLOCKS * LANES - D), BF16)], axis=1
    )


def pack_kernel(
    gr0_ref, gr1_ref, gr2_ref, wh0_ref, wh1_ref, wh2_ref, low_ref, rid_ref, slot_ref, core_ref,
    msg_out, all_out, g_hot_out,
):
    relations = [gr0_ref[...], gr1_ref[...], gr2_ref[...]]
    weights = [wh0_ref[...], wh1_ref[...], wh2_ref[...]]
    rel_ids = rid_ref[...]
    place = lax.broadcasted_iota(jnp.int32, (16, LANES), 0)
    for b in range(6):
        ids = rel_ids[:, b * LANES : (b + 1) * LANES]
        high = jnp.right_shift(ids, 6).astype(F32)
        low = jnp.bitwise_and(ids, 63).astype(F32)
        tail = jnp.where(place == 0, high, jnp.where(place == 1, low, 0.0)).astype(BF16)
        piece = relations[b // 2][:, (b % 2) * LANES : (b % 2 + 1) * LANES]
        msg_out[b * REL_ROWS : b * REL_ROWS + D, :] = piece
        all_out[:, b * LANES : (b + 1) * LANES] = piece
        msg_out[b * REL_ROWS + D : (b + 1) * REL_ROWS, :] = tail
    g_hot = dot(low_ref[...], jnp.concatenate(weights, axis=0)).astype(BF16)
    g_hot_out[...] = g_hot
    hot_rows(g_hot, slot_ref[...], 1 - core_ref[0], msg_out, HOT_BASE)


def tail_kernel(
    own_ref, gs0_ref, gs2_ref, sid_ref, g_hot_ref, slot_ref, core_ref, own_out, hot_out
):
    ids = sid_ref[...]
    total = own_ref[...]
    for k, gs_ref in ((0, gs0_ref), (2, gs2_ref)):
        total = total + dot_nt(gs_ref[...], onehot(ENT, ids[:, k * EDGES : (k + 1) * EDGES]))
    own_out[...] = total
    hot_rows(g_hot_ref[...], slot_ref[...], core_ref[0], hot_out, 0)


def spread_kernel(grad_ref, rid_ref, got_ref, hot_ref, core_ref, out_ref, grads, id_ref, slabs, sems):
    edges = grad_ref.shape[1]
    grads[:, :edges] = grad_ref[...]
    id_ref[:, :edges] = rid_ref[...]
    for b in range(6):
        col = edges + b * LANES
        grads[:, col : col + LANES] = got_ref[b * REL_ROWS : b * REL_ROWS + D, :]
        tail = got_ref[b * REL_ROWS + D : (b + 1) * REL_ROWS, :].astype(F32)
        ids = tail[0:1] * 64.0 + tail[1:2]
        id_ref[:, col : col + LANES] = ids.astype(jnp.int32)
    ids = id_ref[...] - core_ref[0] * (NREL // 2)
    copies = []
    for i in range(NREL // 2 // SPREAD):
        wide = dot_nt(grads[...], onehot(SPREAD, ids - i * SPREAD))
        count = SPREAD // LANES
        for n in range(count):
            for zl in range(2):
                j = 2 * count * i + 4 * (n // 2) + 2 * zl + n % 2
                hot = []
                for b in range(HOT_BLOCKS):
                    row = b * 512 + j * 16
                    hot.append(
                        hot_ref[row : row + 16, :].astype(F32)
                        + got_ref[HOT_BASE + row : HOT_BASE + row + 16, :].astype(F32)
                    )
                last = hot.pop()
                tail = jnp.concatenate(
                    [last[:8, :16], last[8:, :16], jnp.zeros((8, LANES - 32), F32)], axis=1
                )
                piece = wide[zl * HALF_D : (zl + 1) * HALF_D, n * LANES : (n + 1) * LANES]
                slabs[j] = jnp.concatenate([piece, tail] + hot, axis=0).astype(BF16)
        part = pl.ds(2 * count * i, 2 * count)
        copy = pltpu.make_async_copy(slabs.at[part], out_ref.at[part], sems.at[i])
        copy.start()
        copies.append(copy)
    for copy in copies:
        copy.wait()


def near_sum_kernel(in_ref, out_ref):
    total = in_ref[0].astype(F32)
    for j in range(1, GROUP):
        total = total + in_ref[j].astype(F32)
    out_ref[...] = total.astype(BF16)


def pair_sum_kernel(mine_ref, got_ref, out_ref):
    out_ref[...] = (mine_ref[...].astype(F32) + got_ref[...].astype(F32)).astype(BF16)


def quad_sum_kernel(mine_ref, got_ref, place_ref, rel_ref, hot_ref):
    place = place_ref[0]
    total = mine_ref[...].astype(F32) + got_ref[...].astype(F32)
    rel = total[:HALF_D].astype(BF16)
    for j in range(GROUP):
        rel_ref[j] = rel
    for q in range(QUAD):

        @pl.when(place == q)
        def _():
            for b in range(3):
                row = HOT_AT + b * 16 + q * 4
                hot_ref[:, b * LANES : (b + 1) * LANES] = total[row : row + 4]
            row, col = TAIL + (q % 2) * 4, (q // 2) * 16
            hot_ref[:, 3 * LANES :] = total[row : row + 4, col : col + 16]


def merge_kernel(core_ref, in_ref, *refs):
    out_ref = refs[-1]
    for near in range(in_ref.shape[0] // 4):
        for zl in range(2):
            for rep in range(2):
                col = (2 * near + rep) * LANES
                out_ref[zl * HALF_D : (zl + 1) * HALF_D, col : col + LANES] = in_ref[
                    4 * near + 2 * zl + rep
                ].astype(F32)


def merged(core, value, before):
    steps = GROUP // 16
    first = before is None
    if first:
        place = lambda i, c: (0, c[0] * steps + i)
    else:
        place = lambda i, c: (0, (1 - c[0]) * steps + i)
    in_specs = [pl.BlockSpec((16, HALF_D, LANES), lambda i, c: (i, 0, 0))]
    if not first:
        in_specs.append(pl.BlockSpec(memory_space=pl.ANY))
    return pl.pallas_call(
        merge_kernel,
        out_shape=struct((D, NREL), F32),
        grid_spec=pltpu.PrefetchScalarGridSpec(
            num_scalar_prefetch=1,
            grid=(steps,),
            in_specs=in_specs,
            out_specs=pl.BlockSpec((D, 8 * LANES), place),
        ),
        input_output_aliases={} if first else {2: 0},
        compiler_params=PARAMS,
        cost_estimate=pl.CostEstimate(flops=0, bytes_accessed=10**7, transcendentals=0),
        name="merge",
    )(core, value, *([] if first else [before]))


def struct(shape, dtype):
    return jax.ShapeDtypeStruct(shape, dtype)


COST = pl.CostEstimate(flops=10**8, bytes_accessed=10**6, transcendentals=0)
PARAMS = pltpu.CompilerParams(vmem_limit_bytes=28 * 1024 * 1024)
VMEM = pl.BlockSpec(memory_space=pltpu.VMEM)
SMEM = pl.BlockSpec(memory_space=pltpu.SMEM)
HBM = pl.BlockSpec(memory_space=pltpu.HBM)


def moved(value, axis, count, steps):
    return lax.ppermute(value, axis, [(i, (i + steps) % count) for i in range(count)])


def shards(entities, hot_entities, relations, src_ids, rel_ids, dst_ids, neg_ids, counts, hot_slot):
    blocks = lax.axis_size(BLK)
    own = entities.T
    hot = hot_entities.T
    rel = relations.T
    sid = src_ids.reshape(1, -1)
    rid = rel_ids.reshape(1, -1)
    did = dst_ids.reshape(1, -1)
    nid = neg_ids.reshape(1, -1)
    count = counts.reshape(-1)
    slot = hot_slot.reshape(1, -1)
    core = lax.axis_index("core").astype(jnp.int32).reshape(1)
    after = moved(own, BLK, blocks, -1)
    before = moved(own, BLK, blocks, 1)
    edges = sid.shape[1]
    relg = pl.pallas_call(
        lookup_kernel,
        out_shape=struct((D, edges), BF16),
        in_specs=[VMEM, VMEM],
        out_specs=VMEM,
        compiler_params=PARAMS,
        cost_estimate=pl.CostEstimate(flops=3 * 10**9, bytes_accessed=10**7, transcendentals=0),
        name="lookup",
    )(rel, rid)
    half = struct((D, EDGES), BF16)
    block = struct((D, ENT), BF16)
    weight = struct((EDGES, HOT), BF16)
    src, low, low_t, gr1, own_grad, wh1 = pl.pallas_call(
        front_kernel,
        out_shape=(
            struct((D, edges), BF16), struct((D, edges), BF16), struct((edges, D), BF16),
            half, struct((D, ENT), F32), weight,
        ),
        in_specs=[VMEM] * 6 + [SMEM],
        out_specs=[VMEM] * 6,
        compiler_params=PARAMS,
        cost_estimate=COST,
        name="front",
    )(relg, own, hot, sid, did, nid, count)

    def back(k, far):
        return pl.pallas_call(
            functools.partial(back_kernel, k),
            out_shape=(half, half, weight, block),
            in_specs=[VMEM] * 8 + [SMEM],
            out_specs=[VMEM] * 4,
            compiler_params=PARAMS,
            cost_estimate=COST,
            name="back",
        )(far, hot, src, relg, low, low_t, did, nid, count)

    gs0, gr0, wh0, next_grad = back(0, after)
    from_prev = moved(next_grad, BLK, blocks, 1)
    gs2, gr2, wh2, prev_grad = back(2, before)
    from_next = moved(prev_grad, BLK, blocks, -1)
    msg, grads, g_hot = pl.pallas_call(
        pack_kernel,
        out_shape=(
            struct((MSG_ROWS, LANES), BF16), struct((D, edges), BF16),
            struct((D, HOT), BF16),
        ),
        in_specs=[VMEM] * 9 + [SMEM],
        out_specs=[VMEM] * 3,
        compiler_params=PARAMS,
        cost_estimate=COST,
        name="pack",
    )(gr0, gr1, gr2, wh0, wh1, wh2, low, rid, slot, core)
    own_grad, hot_mine = pl.pallas_call(
        tail_kernel,
        out_shape=(struct((D, ENT), F32), struct((HOT_BLOCKS * 512, LANES), BF16)),
        in_specs=[VMEM] * 6 + [SMEM],
        out_specs=[VMEM] * 2,
        compiler_params=PARAMS,
        cost_estimate=COST,
        name="tail",
    )(own_grad, gs0, gs2, sid, g_hot, slot, core)
    swap = [(0, 1), (1, 0)]
    got = lax.ppermute(msg, "core", swap)
    got, own_grad, hot_mine = lax.optimization_barrier((got, own_grad, hot_mine))
    slabs = pl.pallas_call(
        spread_kernel,
        out_shape=struct((GROUP, SLAB, LANES), BF16),
        in_specs=[VMEM] * 4 + [SMEM],
        out_specs=HBM,
        scratch_shapes=[
            pltpu.VMEM((D, 2 * edges), BF16),
            pltpu.VMEM((1, 2 * edges), jnp.int32),
            pltpu.VMEM((GROUP, SLAB, LANES), BF16),
            pltpu.SemaphoreType.DMA((NREL // 2 // SPREAD,)),
        ],
        compiler_params=PARAMS,
        cost_estimate=COST,
        name="spread",
    )(grads, rid, got, hot_mine, core)
    slabs, from_prev, from_next = lax.optimization_barrier((slabs, from_prev, from_next))
    slabs = lax.all_to_all(slabs, NEAR, 0, 0, tiled=True)
    part = (own_grad + from_prev.astype(F32) + from_next.astype(F32)).astype(BF16)
    slabs, part = lax.optimization_barrier((slabs, part))
    twin = lax.ppermute(part, "rep", swap)
    pieces = pl.pallas_call(
        near_sum_kernel,
        out_shape=struct((SLAB, LANES), BF16),
        in_specs=[VMEM],
        out_specs=VMEM,
        compiler_params=PARAMS,
        name="near_sum",
    )(slabs)
    beside = lax.ppermute(pieces, "zh", [(i, i ^ 1) for i in range(QUAD)])
    pieces = pl.pallas_call(
        pair_sum_kernel,
        out_shape=struct((SLAB, LANES), BF16),
        in_specs=[VMEM] * 2,
        out_specs=VMEM,
        compiler_params=PARAMS,
        name="pair_sum",
    )(pieces, beside)
    across = lax.ppermute(pieces, "zh", [(i, i ^ 3) for i in range(QUAD)])
    place = lax.axis_index("zh").astype(jnp.int32).reshape(1)
    column, hot_grad = pl.pallas_call(
        quad_sum_kernel,
        out_shape=(struct((GROUP, HALF_D, LANES), BF16), struct((4, D), F32)),
        in_specs=[VMEM] * 2 + [SMEM],
        out_specs=(VMEM, VMEM),
        compiler_params=PARAMS,
        name="quad_sum",
    )(pieces, across, place)
    column, twin = lax.optimization_barrier((column, twin))
    mine = lax.all_to_all(column, NEAR, 0, 0, tiled=True)
    other = lax.ppermute(mine, "core", swap)
    relation_grad = merged(core, other, merged(core, mine, None))
    entity_grad = part.astype(F32) + twin.astype(F32)
    return entity_grad.T, relation_grad.T, hot_grad


def solution(mesh):
    inner = Mesh(mesh.devices.reshape(4, 2, 4, 2, 2, 2), BLK + ("rep",))
    return jax.shard_map(
        shards,
        mesh=inner,
        in_specs=(
            P(BLK, None),
            P(),
            P(),
            P(BLK, "rep", None, None),
            P(BLK, "rep", None, None),
            P(BLK, "rep", None, None),
            P(BLK, "rep", None, None),
            P(BLK, "rep", None),
            P(),
        ),
        out_specs=(P(BLK, None), P(), P(BLK + ("rep",), None)),
        check_vma=False,
    )
```
